32 devices in a mesh: ch: 32 (over z, y, x, core).
Axes of the slice: x: 2, y: 2, z: 4, core: 2. Of those that a mesh axis runs over, the one named last changes fastest.
Arguments:
- spectra: bfloat16 [4, 16384, 128], P(None, 'ch'), may hold values from -6 to 6
- offsets: int32 [16384], P('ch'), may hold values from 0 to 7
- bins: int32 [4], replicated, may hold values from 1 to 63
Outputs:
- gradient: float32 [4, 16384, 128], P(None, 'ch')
The draws below stay inside these ranges and needn't reach their ends.
All inputs are finite; a program needn't handle non-finite values.
Results may differ from the reference program's by a relative error of at most 0.0015.
Values may be sent and summed in bfloat16 or wider, within the bound.
No kernel may reach another device: no remote copies, remote signals or barrier semaphores. Data moves between devices by JAX's collectives and lax.ppermute only.
A program may use at most 64 MiB of HBM per device.

```python
import math
import jax
import jax.numpy as jnp
from jax import lax

C_DEV = 512
WIN = 64
F = 4
NEXT = 3
NC = 16384
N_CH = 32


def plant(array, own_key, low, high):
    spot = [jax.random.randint(jax.random.fold_in(own_key, axis), (), 0, length) for axis, length in enumerate(array.shape)]
    longest = array.shape.index(max(array.shape))
    neighbour = spot[:longest] + [(spot[longest] + 1) % array.shape[longest]] + spot[longest + 1:]
    return array.at[tuple(spot)].set(low).at[tuple(neighbour)].set(high)


def steps_of(stream_key, shape, split, low, top_value):
    def one(dim, parts):
        draws = jax.random.uniform(jax.random.fold_in(jax.random.fold_in(stream_key, 6), dim), (parts,), jnp.float32, low / len(split), top_value / len(split))
        return jnp.repeat(jnp.exp(draws), shape[dim] // parts).reshape((-1,) + (1,) * (len(shape) - dim - 1))

    gain = one(*split[0])
    for cut in split[1:]:
        gain = gain * one(*cut)
    return gain


def centred(rng, shape, scale, reach, shards=(), kind=jnp.bfloat16):
    loudness = steps_of(rng, shape, shards, -0.22, 0.18) if shards else 1.0
    values = jax.random.normal(rng, shape, jnp.float32) * scale * loudness
    return jnp.minimum(jnp.maximum(values, -reach), reach).astype(kind)


def setup_inputs(seed: int = 0) -> dict:
    key_list = jax.random.split(jax.random.key(seed), 4)
    return {
        "spectra": centred(key_list[0], (F, NC, 2 * WIN), 1.0, 6.0, ((1, 32),)),
        "offsets": plant(jax.random.randint(key_list[1], (NC,), 0, 8), jax.random.fold_in(key_list[1], 1), 0, 7).astype(jnp.int32),
        "bins": plant(jax.random.randint(key_list[2], (F,), 1, 64), jax.random.fold_in(key_list[2], 1), 1, 63).astype(jnp.int32),
    }


spacing_metres = 8
period_metres = 4096
model_amp = 0.5


def block_terms(mine, mine_off, other, other_off, gap, bins):
    windows = mine.shape[2] // 2
    channels = mine.shape[1]
    mine_f = mine.astype(jnp.float32)
    other_f = other.astype(jnp.float32)
    other_swap = jnp.concatenate([-other_f[..., windows:], other_f[..., :windows]], axis=-1)
    mine_swap = jnp.concatenate([mine_f[..., windows:], -mine_f[..., :windows]], axis=-1)
    real_part = jnp.einsum("fik,fjk->fij", mine_f, other_f) / windows
    imag_part = jnp.einsum("fik,fjk->fij", mine_f, other_swap) / windows
    rows = jnp.arange(channels, dtype=jnp.int32)
    distance = (gap + rows[None, :] - rows[:, None]) * spacing_metres + other_off[None, :] - mine_off[:, None]
    wrapped = jnp.mod(bins[:, None, None] * distance[None, :, :], period_metres)
    phase = wrapped.astype(jnp.float32) * (2.0 * math.pi / period_metres)
    grad_real = jnp.tanh(real_part - model_amp * jnp.cos(phase)).astype(jnp.bfloat16).astype(jnp.float32)
    grad_imag = jnp.tanh(imag_part - model_amp * jnp.sin(phase)).astype(jnp.bfloat16).astype(jnp.float32)
    forward_term = jnp.einsum("fij,fjk->fik", grad_real, other_f) + jnp.einsum("fij,fjk->fik", grad_imag, other_swap)
    back_term = jnp.einsum("fij,fik->fjk", grad_real, mine_f) + jnp.einsum("fij,fik->fjk", grad_imag, mine_swap)
    return forward_term, back_term


def reference(spectra, offsets, bins):
    nblocks = N_CH
    channels = C_DEV
    freqs = spectra.shape[0]
    width = spectra.shape[2]
    blocks = spectra.reshape(freqs, nblocks, channels, width).transpose(1, 0, 2, 3)
    blocks = jnp.concatenate([blocks, jnp.zeros((NEXT, freqs, channels, width), blocks.dtype)], axis=0)
    off_blocks = offsets.reshape(nblocks, channels)
    off_blocks = jnp.concatenate([off_blocks, jnp.zeros((NEXT, channels), jnp.int32)], axis=0)

    def one_block(index):
        mine = blocks[index]
        mine_off = off_blocks[index]
        total = jnp.zeros((freqs, channels, width), jnp.float32)
        backs = []
        for distance in range(NEXT + 1):
            other = lax.dynamic_index_in_dim(blocks, (index + distance).astype(jnp.int32), 0, keepdims=False)
            other_off = lax.dynamic_index_in_dim(off_blocks, (index + distance).astype(jnp.int32), 0, keepdims=False)
            forward_term, back_term = block_terms(mine, mine_off, other, other_off, distance * channels, bins)
            total = total + forward_term
            backs.append(back_term)
        return total, jnp.stack(backs)

    forward_all, back_all = lax.map(one_block, jnp.arange(nblocks, dtype=jnp.int32))
    result = forward_all
    for distance in range(NEXT + 1):
        moved = jnp.concatenate([jnp.zeros((distance, freqs, channels, width), jnp.float32), back_all[:, distance]], axis=0)[:nblocks]
        result = result + moved
    result = result / (width // 2)
    return result.transpose(1, 0, 2, 3).reshape(freqs, nblocks * channels, width)
```

```python
import functools
import math

import jax
import jax.numpy as jnp
from jax import lax
from jax.experimental import pallas as pl
from jax.experimental.pallas import tpu as pltpu
from jax.sharding import PartitionSpec as P

spacing_metres = 8
period_metres = 4096
model_amp = 0.5
reach = 3

OWN = (0, 0)
PAIR = (1, -1)
NEXT = (2, 2)
PREV = (-2, -2)
FAR = (-3, 3)
NEXT_OF_PAIR = (3, 1)
PREV_OF_PAIR = (-1, -3)


def sine(steps):
    half, quarter = period_metres // 2, period_metres // 4
    turn = jnp.bitwise_and(steps + half, period_metres - 1) - half
    turn = jnp.where(turn > quarter, half - turn, jnp.where(turn < -quarter, -half - turn, turn))
    x = turn.astype(jnp.float32) * (2.0 * math.pi / period_metres)
    square = x * x
    total = jnp.full_like(x, -1.0 / math.factorial(11))
    for order in (9, 7, 5, 3, 1):
        total = total * square + (-1.0) ** (order // 2) / math.factorial(order)
    return total * x


def halves(value):
    high = value.astype(jnp.bfloat16).astype(jnp.float32)
    return high, value - high


def rows_of(freqs):
    return -(-2 * freqs // 8) * 8


def angles(bins_ref, off_ref, block, freqs, channels):
    shape = (rows_of(freqs), channels)
    row = lax.broadcasted_iota(jnp.int32, shape, 0)
    offsets = off_ref[...].astype(jnp.float32)
    lines = channels // offsets.shape[1]
    offsets = jnp.concatenate([offsets[i : i + 1] for i in range(lines)], axis=1).astype(jnp.int32)
    channel = lax.broadcasted_iota(jnp.int32, shape, 1) + block * channels
    pos = channel * spacing_metres + offsets
    factor = jnp.zeros(shape, jnp.int32)
    for f in range(freqs):
        factor = jnp.where((row == f) | (row == freqs + f), bins_ref[f], factor)
    return factor * pos, row < freqs


def columns(parts, width):
    rows = jnp.concatenate(parts, axis=0)
    rows = jnp.concatenate(
        [rows, jnp.zeros((width - rows.shape[0], rows.shape[1]), jnp.float32)], axis=0
    )
    return rows.T.astype(jnp.bfloat16)


def key_columns(bins_ref, off_ref, block, freqs, channels, width):
    angle, is_cos = angles(bins_ref, off_ref, block, freqs, channels)
    high, low = halves(sine(angle + jnp.where(is_cos, period_metres // 4, 0)))
    return columns([high, low, high, low], width)


def query_columns(bins_ref, off_ref, block, freqs, channels, width):
    angle, is_cos = angles(bins_ref, off_ref, block, freqs, channels)
    quarter = period_metres // 4
    high, low = halves(-model_amp * sine(angle + jnp.where(is_cos, quarter, 0)))
    real = columns([high, high, low, low], width)
    high, low = halves(model_amp * sine(angle - jnp.where(is_cos, 0, quarter)))
    imag = columns([high, high, low, low], width)
    return real, imag


def turned(value):
    width = value.shape[1]
    lane = lax.broadcasted_iota(jnp.int32, value.shape, 1)
    moved = pltpu.roll(value, width // 2, 1)
    return jnp.where(lane < width // 2, -moved, moved)


def band_kernel(freqs, places, weight, axis, has_total, *refs):
    count = len(places)
    bins_ref, own_ref, own_off_ref = refs[:3]
    key_refs = refs[3 : 3 + 2 * count]
    total_ref = refs[3 + 2 * count] if has_total else None
    out_ref, query_ref = refs[3 + 2 * count + has_total :]
    width = own_ref.shape[1]
    channels = out_ref.shape[1]
    windows = width // 2
    me = lax.axis_index(axis)
    odd = lax.rem(me, 2)
    real, imag = query_columns(bins_ref, own_off_ref, me, freqs, channels, width)
    lane = lax.broadcasted_iota(jnp.int32, (channels, width), 1)
    period = rows_of(freqs)
    lane_row = lax.rem(lane, period)
    used = lane < 4 * period
    extra = []
    for (even_step, odd_step), off_ref in zip(places, key_refs[1::2]):
        block = me + even_step + odd * (odd_step - even_step)
        extra.append(key_columns(bins_ref, off_ref, block, freqs, channels, width))
    zero = jnp.zeros((), jnp.bfloat16)
    for f in range(freqs):
        rows = pl.ds(f * channels, channels)
        own = own_ref[rows, :].astype(jnp.float32) / windows
        mine = used & ((lane_row == f) | (lane_row == freqs + f))
        query_ref[f, :channels, :width] = own.astype(jnp.bfloat16)
        query_ref[f, channels:, :width] = (-turned(own)).astype(jnp.bfloat16)
        query_ref[f, :channels, width:] = jnp.where(mine, real, zero)
        query_ref[f, channels:, width:] = jnp.where(mine, imag, zero)
    for f in range(freqs):
        rows = pl.ds(f * channels, channels)
        sums = []
        for half in range(2):
            query = query_ref[f, pl.ds(half * channels, channels), :]
            part = None
            for key_ref, columns_j in zip(key_refs[0::2], extra):
                key = key_ref[rows, :]
                misfit = lax.dot_general(
                    query,
                    jnp.concatenate([key, columns_j], axis=1),
                    (((1,), (1,)), ((), ())),
                    preferred_element_type=jnp.float32,
                )
                grad = jnp.tanh(misfit).astype(jnp.bfloat16)
                term = jnp.dot(grad, key, preferred_element_type=jnp.float32)
                part = term if part is None else part + term
            sums.append(part)
        term = (sums[0] + turned(sums[1])) * (weight / windows)
        if has_total:
            term = term + total_ref[f]
        out_ref[f] = term


def band_terms(shape, axis, bins, own, keys, places, weight=1, total=None):
    freqs, channels, width = shape
    tail_rows = own.shape[0] - freqs * channels
    whole = pl.BlockSpec((freqs * channels, width), lambda i: (0, 0))
    tail = pl.BlockSpec((tail_rows, width), lambda i: (freqs * channels // tail_rows, 0))
    plain = pl.BlockSpec((freqs, channels, width), lambda i: (0, 0, 0))
    has_total = total is not None
    operands = [bins, own, own]
    specs = [pl.BlockSpec(memory_space=pltpu.SMEM), whole, tail]
    for key in keys:
        operands += [key, key]
        specs += [whole, tail]
    if has_total:
        operands.append(total)
        specs.append(plain)
    pairs = len(keys) * freqs * channels * channels
    return pl.pallas_call(
        functools.partial(band_kernel, freqs, tuple(places), weight, axis, has_total),
        grid=(1,),
        out_shape=jax.ShapeDtypeStruct(shape, jnp.float32),
        in_specs=specs,
        out_specs=plain,
        scratch_shapes=[pltpu.VMEM((freqs, 2 * channels, 2 * width), jnp.bfloat16)],
        input_output_aliases={len(operands) - 1: 0} if has_total else {},
        compiler_params=pltpu.CompilerParams(vmem_limit_bytes=40 << 20),
        cost_estimate=pl.CostEstimate(
            flops=16 * pairs * width, bytes_accessed=1 << 21, transcendentals=2 * pairs
        ),
    )(*operands)


def local(axis, count, spectra, offsets, bins):
    shape = spectra.shape
    freqs, channels, width = shape

    def moved(value, target):
        pairs = [(i, target(i)) for i in range(count)]
        return lax.ppermute(value, axis, [(i, t) for i, t in pairs if 0 <= t < count])

    lines = channels // width
    tail = jnp.zeros((-(-lines // 16) * 16, width), jnp.bfloat16)
    tail = tail.at[:lines].set(offsets.astype(jnp.bfloat16).reshape(lines, width))
    own = jnp.concatenate([spectra.reshape(freqs * channels, width), tail], axis=0)

    nxt = moved(own, lambda i: i - 2)
    prev = moved(own, lambda i: i + 2)
    far = moved(own, lambda i: i + 3 if i % 2 else i - 3)
    pair = moved(own, lambda i: i ^ 1)
    nxt_pair = moved(nxt, lambda i: i ^ 1)
    prev_pair = moved(prev, lambda i: i ^ 1)

    terms = functools.partial(band_terms, shape, axis, bins, own)
    total = terms([own], [OWN], weight=2)
    total = terms([pair], [PAIR], total=total)
    total = terms([nxt], [NEXT], total=total)
    total = terms([nxt_pair, far], [NEXT_OF_PAIR, FAR], total=total)
    total = terms([prev], [PREV], total=total)
    total = terms([prev_pair], [PREV_OF_PAIR], total=total)
    return total


def solution(mesh):
    (axis,) = mesh.axis_names
    return jax.shard_map(
        functools.partial(local, axis, mesh.shape[axis]),
        mesh=mesh,
        in_specs=(P(None, axis, None), P(axis), P()),
        out_specs=P(None, axis, None),
        check_vma=False,
    )
```

```python
import functools
import math

import jax
import jax.numpy as jnp
from jax import lax
from jax.experimental import pallas as pl
from jax.experimental.pallas import tpu as pltpu
from jax.sharding import PartitionSpec as P

spacing_metres = 8
period_metres = 4096
model_amp = 0.5
vmem = 24 << 20

OWN = (0, 0)
PAIR = (1, -1)
NEXT = (2, 2)
PREV = (-2, -2)
FAR = (-3, 3)
NEXT_OF_PAIR = (3, 1)
PREV_OF_PAIR = (-1, -3)


def sine(steps):
    half, quarter = period_metres // 2, period_metres // 4
    turn = jnp.bitwise_and(steps + half, period_metres - 1) - half
    turn = jnp.where(turn > quarter, half - turn, jnp.where(turn < -quarter, -half - turn, turn))
    x = turn.astype(jnp.float32) * (2.0 * math.pi / period_metres)
    square = x * x
    total = jnp.full_like(x, -1.0 / math.factorial(11))
    for order in (9, 7, 5, 3, 1):
        total = total * square + (-1.0) ** (order // 2) / math.factorial(order)
    return total * x


def halves(value):
    high = value.astype(jnp.bfloat16).astype(jnp.float32)
    return high, value - high


def rows_of(freqs):
    return -(-2 * freqs // 8) * 8


def angles(tail_ref, block, freqs, channels):
    rows, width = rows_of(freqs), tail_ref.shape[1]
    row = lax.broadcasted_iota(jnp.int32, (rows, channels), 0)
    tail = tail_ref[...].astype(jnp.float32)
    lines = channels // width
    offsets = jnp.concatenate([tail[i : i + 1] for i in range(lines)], axis=1).astype(jnp.int32)
    factor = jnp.concatenate([tail[-rows:]] * lines, axis=1).astype(jnp.int32)
    channel = lax.broadcasted_iota(jnp.int32, (rows, channels), 1) + block * channels
    return factor * (channel * spacing_metres + offsets), row < freqs


def columns(parts, width):
    rows = jnp.concatenate(parts, axis=0)
    rows = jnp.concatenate(
        [rows, jnp.zeros((width - rows.shape[0], rows.shape[1]), jnp.float32)], axis=0
    )
    return rows.T.astype(jnp.bfloat16)


def key_columns(tail_ref, block, freqs, channels, width):
    angle, is_cos = angles(tail_ref, block, freqs, channels)
    high, low = halves(sine(angle + jnp.where(is_cos, period_metres // 4, 0)))
    return columns([high, low, high, low], width)


def query_columns(tail_ref, block, freqs, channels, width):
    angle, is_cos = angles(tail_ref, block, freqs, channels)
    quarter = period_metres // 4
    high, low = halves(-model_amp * sine(angle + jnp.where(is_cos, quarter, 0)))
    real = columns([high, high, low, low], width)
    high, low = halves(model_amp * sine(angle - jnp.where(is_cos, 0, quarter)))
    imag = columns([high, high, low, low], width)
    return real, imag


def turned(value):
    width = value.shape[1]
    lane = lax.broadcasted_iota(jnp.int32, value.shape, 1)
    moved = pltpu.roll(value, width // 2, 1)
    return jnp.where(lane < width // 2, -moved, moved)


def block_of(axis, place):
    me = lax.axis_index(axis)
    return me + place[0] + lax.rem(me, 2) * (place[1] - place[0])


def pack_kernel(spectra_ref, off_ref, bins_ref, out_ref, off, bins, sems):
    rows, width = spectra_ref.shape
    freqs = bins_ref.shape[0]
    sources, targets = (spectra_ref, off_ref, bins_ref), (out_ref.at[pl.ds(0, rows)], off, bins)
    copies = [pltpu.make_async_copy(a, b, sems.at[i]) for i, (a, b) in enumerate(zip(sources, targets))]
    for copy in copies:
        copy.start()
    for copy in copies[1:]:
        copy.wait()
    tail = (out_ref.shape[0] - rows, width)
    row = lax.broadcasted_iota(jnp.int32, tail, 0)
    value = jnp.zeros(tail, jnp.int32)
    for i in range(off.shape[1] // width):
        value = jnp.where(row == i, off[:, i * width : (i + 1) * width], value)
    first = tail[0] - rows_of(freqs)
    for f in range(freqs):
        value = jnp.where((row == first + f) | (row == first + freqs + f), bins[f], value)
    out_ref[rows:, :] = value.astype(jnp.float32).astype(jnp.bfloat16)
    copies[0].wait()


def pack(spectra, offsets, bins):
    freqs, channels, width = spectra.shape
    tail = -(-(channels // width + rows_of(freqs)) // 16) * 16
    return pl.pallas_call(
        pack_kernel,
        out_shape=jax.ShapeDtypeStruct((freqs * channels + tail, width), spectra.dtype),
        in_specs=[pl.BlockSpec(memory_space=pltpu.HBM)] * 3,
        out_specs=pl.BlockSpec(memory_space=pltpu.VMEM),
        scratch_shapes=[
            pltpu.VMEM((1, channels), jnp.int32),
            pltpu.SMEM((freqs,), jnp.int32),
            pltpu.SemaphoreType.DMA((3,)),
        ],
        compiler_params=pltpu.CompilerParams(vmem_limit_bytes=vmem),
        cost_estimate=pl.CostEstimate(flops=0, bytes_accessed=1 << 20, transcendentals=0),
    )(
        *(
            pltpu.with_memory_space_constraint(value, pltpu.HBM)
            for value in (spectra.reshape(freqs * channels, width), offsets.reshape(1, channels), bins)
        )
    )


def fill_queries(own_ref, query_ref, block):
    freqs, channels, width = query_ref.shape[0], query_ref.shape[1] // 2, own_ref.shape[1]
    windows = width // 2
    real, imag = query_columns(
        own_ref.at[pl.ds(freqs * channels, own_ref.shape[0] - freqs * channels)],
        block,
        freqs,
        channels,
        width,
    )
    lane = lax.broadcasted_iota(jnp.int32, (channels, width), 1)
    lane_row = lax.rem(lane, rows_of(freqs))
    used = lane < 4 * rows_of(freqs)
    zero = jnp.zeros((), jnp.bfloat16)
    for f in range(freqs):
        own = own_ref[pl.ds(f * channels, channels), :].astype(jnp.float32) / windows
        mine = used & ((lane_row == f) | (lane_row == freqs + f))
        query_ref[f, :channels, :width] = own.astype(jnp.bfloat16)
        query_ref[f, channels:, :width] = (-turned(own)).astype(jnp.bfloat16)
        query_ref[f, :channels, width:] = jnp.where(mine, real, zero)
        query_ref[f, channels:, width:] = jnp.where(mine, imag, zero)


def band_sums(query_ref, keys, f, extra):
    channels, width = query_ref.shape[1] // 2, query_ref.shape[2] // 2
    sums = []
    for half in range(2):
        query = query_ref[f, pl.ds(half * channels, channels), :]
        part = None
        for key_ref, columns_j in zip(keys, extra):
            key = key_ref[pl.ds(f * channels, channels), :]
            misfit = lax.dot_general(
                query,
                jnp.concatenate([key, columns_j], axis=1),
                (((1,), (1,)), ((), ())),
                preferred_element_type=jnp.float32,
            )
            grad = jnp.tanh(misfit).astype(jnp.bfloat16)
            term = jnp.dot(grad, key, preferred_element_type=jnp.float32)
            part = term if part is None else part + term
        sums.append(part)
    return sums[0] + turned(sums[1])


def columns_of(key_ref, block, freqs, channels, width):
    tail_ref = key_ref.at[pl.ds(freqs * channels, key_ref.shape[0] - freqs * channels)]
    return key_columns(tail_ref, block, freqs, channels, width)


def own_kernel(axis, own_ref, query_ref, total_ref):
    freqs, channels, width = total_ref.shape
    block = block_of(axis, OWN)
    extra = columns_of(own_ref, block, freqs, channels, width)
    fill_queries(own_ref, query_ref, block)
    for f in range(freqs):
        term = band_sums(query_ref, [own_ref], f, [extra])
        total_ref[f] = term * (4.0 / width)


def band_kernel(axis, places, last, query_ref, *refs):
    keys, (total_ref, out_ref) = refs[: len(places)], refs[len(places) : len(places) + 2]
    freqs, channels, width = total_ref.shape
    extra = [
        columns_of(key_ref, block_of(axis, place), freqs, channels, width)
        for key_ref, place in zip(keys, places)
    ]
    copies = []
    for f in range(freqs):
        term = band_sums(query_ref, keys, f, extra)
        term = total_ref[f] + term * (2.0 / width)
        if last:
            result_ref, sems = refs[len(places) + 2 :]
            result_ref[f] = term
            copies.append(pltpu.make_async_copy(result_ref.at[f], out_ref.at[f], sems.at[f]))
            copies[f].start()
        else:
            out_ref[f] = term
    for copy in copies:
        copy.wait()


def cost(shape, blocks):
    pairs = blocks * shape[0] * shape[1] * shape[1]
    return pl.CostEstimate(
        flops=64 * pairs * shape[2], bytes_accessed=1 << 21, transcendentals=2 * pairs
    )


def own_terms(shape, axis, own):
    freqs, channels, width = shape
    whole = pl.BlockSpec(memory_space=pltpu.VMEM)
    return pl.pallas_call(
        functools.partial(own_kernel, axis),
        out_shape=[
            jax.ShapeDtypeStruct((freqs, 2 * channels, 2 * width), jnp.bfloat16),
            jax.ShapeDtypeStruct(shape, jnp.float32),
        ],
        in_specs=[whole],
        out_specs=[whole, whole],
        compiler_params=pltpu.CompilerParams(vmem_limit_bytes=vmem),
        cost_estimate=cost(shape, 1),
    )(own)


def band_terms(shape, axis, query, total, keys, places, last=False):
    whole = pl.BlockSpec(memory_space=pltpu.VMEM)
    scratch = [pltpu.VMEM(shape, jnp.float32), pltpu.SemaphoreType.DMA((shape[0],))]
    return pl.pallas_call(
        functools.partial(band_kernel, axis, tuple(places), last),
        out_shape=jax.ShapeDtypeStruct(shape, jnp.float32),
        in_specs=[whole] * (len(keys) + 2),
        out_specs=pl.BlockSpec(memory_space=pl.ANY) if last else whole,
        scratch_shapes=scratch if last else [],
        compiler_params=pltpu.CompilerParams(vmem_limit_bytes=vmem),
        cost_estimate=cost(shape, len(keys)),
    )(query, *keys, total)


def local(axis, count, spectra, offsets, bins):
    shape = spectra.shape

    def moved(value, target):
        pairs = [(i, target(i)) for i in range(count)]
        return lax.ppermute(value, axis, [(i, t) for i, t in pairs if 0 <= t < count])

    own = pack(spectra, offsets, bins)
    nxt = moved(own, lambda i: i - 2)
    prev = moved(own, lambda i: i + 2)
    far = moved(own, lambda i: i + 3 if i % 2 else i - 3)
    pair = moved(own, lambda i: i ^ 1)

    query, total = own_terms(shape, axis, own)
    terms = functools.partial(band_terms, shape, axis, query)
    total = terms(total, [pair], [PAIR])
    nxt, total = lax.optimization_barrier((nxt, total))
    nxt_pair = moved(nxt, lambda i: i ^ 1)
    total = terms(total, [nxt], [NEXT])
    total = terms(total, [nxt_pair, far], [NEXT_OF_PAIR, FAR])
    prev, total = lax.optimization_barrier((prev, total))
    prev_pair = moved(prev, lambda i: i ^ 1)
    total = terms(total, [prev], [PREV])
    total = terms(total, [prev_pair], [PREV_OF_PAIR], last=True)
    return total


def solution(mesh):
    (axis,) = mesh.axis_names
    return jax.shard_map(
        functools.partial(local, axis, mesh.shape[axis]),
        mesh=mesh,
        in_specs=(P(None, axis, None), P(axis), P()),
        out_specs=P(None, axis, None),
        check_vma=False,
    )
```

```python
import functools
import math

import jax
import jax.numpy as jnp
from jax import lax
from jax.experimental import pallas as pl
from jax.experimental.pallas import tpu as pltpu
from jax.sharding import PartitionSpec as P

spacing_metres = 8
period_metres = 4096
model_amp = 0.5
vmem = 24 << 20

OWN = (0, 0)
PAIR = (1, -1)
NEAR = (2, -2)
CROSS = (-2, 2)
FAR = (-3, 3)
NEAR_OF_PAIR = (-1, 1)
CROSS_OF_PAIR = (3, -3)


def sine(steps):
    half, quarter = period_metres // 2, period_metres // 4
    turn = jnp.bitwise_and(steps + half, period_metres - 1) - half
    turn = jnp.where(turn > quarter, half - turn, jnp.where(turn < -quarter, -half - turn, turn))
    x = turn.astype(jnp.float32) * (2.0 * math.pi / period_metres)
    square = x * x
    total = jnp.full_like(x, -1.0 / math.factorial(11))
    for order in (9, 7, 5, 3, 1):
        total = total * square + (-1.0) ** (order // 2) / math.factorial(order)
    return total * x


def halves(value):
    high = value.astype(jnp.bfloat16).astype(jnp.float32)
    return high, value - high


def rows_of(freqs):
    return -(-2 * freqs // 8) * 8


def angles(tail_ref, block, freqs, channels):
    rows, width = rows_of(freqs), tail_ref.shape[1]
    row = lax.broadcasted_iota(jnp.int32, (rows, channels), 0)
    tail = tail_ref[...].astype(jnp.float32)
    lines = channels // width
    offsets = jnp.concatenate([tail[i : i + 1] for i in range(lines)], axis=1).astype(jnp.int32)
    factor = jnp.concatenate([tail[-rows:]] * lines, axis=1).astype(jnp.int32)
    channel = lax.broadcasted_iota(jnp.int32, (rows, channels), 1) + block * channels
    return factor * (channel * spacing_metres + offsets), row < freqs


def columns(parts, width):
    rows = jnp.concatenate(parts, axis=0)
    rows = jnp.concatenate(
        [rows, jnp.zeros((width - rows.shape[0], rows.shape[1]), jnp.float32)], axis=0
    )
    return rows.T.astype(jnp.bfloat16)


def key_columns(tail_ref, block, freqs, channels, width):
    angle, is_cos = angles(tail_ref, block, freqs, channels)
    high, low = halves(sine(angle + jnp.where(is_cos, period_metres // 4, 0)))
    return columns([high, low, high, low], width)


def query_columns(tail_ref, block, freqs, channels, width):
    angle, is_cos = angles(tail_ref, block, freqs, channels)
    quarter = period_metres // 4
    high, low = halves(-model_amp * sine(angle + jnp.where(is_cos, quarter, 0)))
    real = columns([high, high, low, low], width)
    high, low = halves(model_amp * sine(angle - jnp.where(is_cos, 0, quarter)))
    imag = columns([high, high, low, low], width)
    return real, imag


def turned(value):
    width = value.shape[1]
    lane = lax.broadcasted_iota(jnp.int32, value.shape, 1)
    moved = pltpu.roll(value, width // 2, 1)
    return jnp.where(lane < width // 2, -moved, moved)


def block_of(axis, place):
    me = lax.axis_index(axis)
    return me + place[0] + lax.rem(me, 2) * (place[1] - place[0])


def pack_kernel(spectra_ref, off_ref, bins_ref, *refs):
    out_refs, (off, bins, sems) = refs[:-3], refs[-3:]
    width = spectra_ref.shape[1]
    freqs, lines = bins_ref.shape[0], off.shape[1] // width
    tail = (-(-(lines + rows_of(freqs)) // 16) * 16, width)
    sources, targets, start = [off_ref, bins_ref], [off, bins], 0
    for out_ref in out_refs:
        rows = out_ref.shape[0] - tail[0]
        sources.append(spectra_ref.at[pl.ds(start, rows)])
        targets.append(out_ref.at[pl.ds(0, rows)])
        start = (start + rows) % spectra_ref.shape[0]
    copies = [
        pltpu.make_async_copy(source, target, sems.at[i])
        for i, (source, target) in enumerate(zip(sources, targets))
    ]
    for copy in copies:
        copy.start()
    for copy in copies[:2]:
        copy.wait()
    row = lax.broadcasted_iota(jnp.int32, tail, 0)
    value = jnp.zeros(tail, jnp.int32)
    for i in range(lines):
        value = jnp.where(row == i, off[:, i * width : (i + 1) * width], value)
    first = tail[0] - rows_of(freqs)
    for f in range(freqs):
        value = jnp.where((row == first + f) | (row == first + freqs + f), bins[f], value)
    for out_ref in out_refs:
        out_ref[out_ref.shape[0] - tail[0] :, :] = value.astype(jnp.float32).astype(jnp.bfloat16)
    for copy in copies[2:]:
        copy.wait()


def pack(spectra, offsets, bins, parts):
    freqs, channels, width = spectra.shape
    tail = -(-(channels // width + rows_of(freqs)) // 16) * 16
    whole = pl.BlockSpec(memory_space=pltpu.VMEM)
    return pl.pallas_call(
        pack_kernel,
        out_shape=[
            jax.ShapeDtypeStruct((part * channels + tail, width), spectra.dtype)
            for part in (freqs, *parts)
        ],
        in_specs=[pl.BlockSpec(memory_space=pltpu.HBM)] * 3,
        out_specs=[whole] * (1 + len(parts)),
        scratch_shapes=[
            pltpu.VMEM((1, channels), jnp.int32),
            pltpu.SMEM((freqs,), jnp.int32),
            pltpu.SemaphoreType.DMA((3 + len(parts),)),
        ],
        compiler_params=pltpu.CompilerParams(vmem_limit_bytes=vmem),
        cost_estimate=pl.CostEstimate(flops=0, bytes_accessed=1 << 20, transcendentals=0),
    )(
        *(
            pltpu.with_memory_space_constraint(value, pltpu.HBM)
            for value in (spectra.reshape(freqs * channels, width), offsets.reshape(1, channels), bins)
        )
    )


def fill_queries(own_ref, query_ref, block):
    freqs, channels, width = query_ref.shape[0], query_ref.shape[1] // 2, own_ref.shape[1]
    windows = width // 2
    real, imag = query_columns(
        own_ref.at[pl.ds(freqs * channels, own_ref.shape[0] - freqs * channels)],
        block,
        freqs,
        channels,
        width,
    )
    lane = lax.broadcasted_iota(jnp.int32, (channels, width), 1)
    lane_row = lax.rem(lane, rows_of(freqs))
    used = lane < 4 * rows_of(freqs)
    zero = jnp.zeros((), jnp.bfloat16)
    for f in range(freqs):
        own = own_ref[pl.ds(f * channels, channels), :].astype(jnp.float32) / windows
        mine = used & ((lane_row == f) | (lane_row == freqs + f))
        query_ref[f, :channels, :width] = own.astype(jnp.bfloat16)
        query_ref[f, channels:, :width] = (-turned(own)).astype(jnp.bfloat16)
        query_ref[f, :channels, width:] = jnp.where(mine, real, zero)
        query_ref[f, channels:, width:] = jnp.where(mine, imag, zero)


def band_sums(query_ref, keys, f, extra, first=0):
    channels, width = query_ref.shape[1] // 2, query_ref.shape[2] // 2
    sums = []
    for half in range(2):
        query = query_ref[f, pl.ds(half * channels, channels), :]
        part = None
        for key_ref, columns_j in zip(keys, extra):
            key = key_ref[pl.ds((f - first) * channels, channels), :]
            misfit = lax.dot_general(
                query,
                jnp.concatenate([key, columns_j], axis=1),
                (((1,), (1,)), ((), ())),
                preferred_element_type=jnp.float32,
            )
            grad = jnp.tanh(misfit).astype(jnp.bfloat16)
            term = jnp.dot(grad, key, preferred_element_type=jnp.float32)
            part = term if part is None else part + term
        sums.append(part)
    return sums[0] + turned(sums[1])


def columns_of(key_ref, block, freqs, channels, width):
    tail = -(-(channels // width + rows_of(freqs)) // 16) * 16
    tail_ref = key_ref.at[pl.ds(key_ref.shape[0] - tail, tail)]
    return key_columns(tail_ref, block, freqs, channels, width)


def chip_kernel(axis, left, own_ref, pair_ref, query_ref, total_ref):
    freqs, channels, width = total_ref.shape
    own, pair = block_of(axis, OWN), block_of(axis, PAIR)
    fill_queries(own_ref, query_ref, own)
    own_columns = columns_of(own_ref, own, freqs, channels, width)
    pair_columns = columns_of(pair_ref, pair, freqs, channels, width)
    for f in range(freqs):
        term = 2.0 * band_sums(query_ref, [own_ref], f, [own_columns])
        if f < freqs - left:
            term = term + band_sums(query_ref, [pair_ref], f, [pair_columns])
        total_ref[f] = term * (2.0 / width)


def band_kernel(axis, places, first, count, last, query_ref, *refs):
    keys, (total_ref, out_ref) = refs[: len(places)], refs[len(places) : len(places) + 2]
    freqs, channels, width = total_ref.shape
    extra = [
        columns_of(key_ref, block_of(axis, place), freqs, channels, width)
        for key_ref, place in zip(keys, places)
    ]
    copies = []
    for f in range(freqs):
        term = total_ref[f]
        if first <= f < first + count:
            term = term + band_sums(query_ref, keys, f, extra, first) * (2.0 / width)
        if last:
            result_ref, sems = refs[len(places) + 2 :]
            result_ref[f] = term
            copies.append(pltpu.make_async_copy(result_ref.at[f], out_ref.at[f], sems.at[f]))
            copies[f].start()
        else:
            out_ref[f] = term
    for copy in copies:
        copy.wait()


def cost(shape, blocks):
    pairs = blocks * shape[0] * shape[1] * shape[1]
    return pl.CostEstimate(
        flops=64 * pairs * shape[2], bytes_accessed=1 << 21, transcendentals=2 * pairs
    )


def chip_terms(shape, axis, own, pair, left):
    freqs, channels, width = shape
    whole = pl.BlockSpec(memory_space=pltpu.VMEM)
    return pl.pallas_call(
        functools.partial(chip_kernel, axis, left),
        out_shape=[
            jax.ShapeDtypeStruct((freqs, 2 * channels, 2 * width), jnp.bfloat16),
            jax.ShapeDtypeStruct(shape, jnp.float32),
        ],
        in_specs=[whole, whole],
        out_specs=[whole, whole],
        compiler_params=pltpu.CompilerParams(vmem_limit_bytes=vmem),
        cost_estimate=cost(shape, 1),
    )(own, pair)


def band_terms(shape, axis, query, total, keys, places, part=None, last=False):
    whole = pl.BlockSpec(memory_space=pltpu.VMEM)
    scratch = [pltpu.VMEM(shape, jnp.float32), pltpu.SemaphoreType.DMA((shape[0],))]
    return pl.pallas_call(
        functools.partial(band_kernel, axis, tuple(places), *(part or (0, shape[0])), last),
        out_shape=jax.ShapeDtypeStruct(shape, jnp.float32),
        in_specs=[whole] * (len(keys) + 2),
        out_specs=pl.BlockSpec(memory_space=pl.ANY) if last else whole,
        scratch_shapes=scratch if last else [],
        compiler_params=pltpu.CompilerParams(vmem_limit_bytes=vmem),
        cost_estimate=cost(shape, len(keys)),
    )(query, *keys, total)


def local(axis, count, spectra, offsets, bins):
    shape = spectra.shape

    def fetched(value, place):
        sources = [(i + place[i % 2], i) for i in range(count)]
        return lax.ppermute(value, axis, [(i, t) for i, t in sources if 0 <= i < count])

    left = shape[0] // 2
    low, high = (0, shape[0] - left), (shape[0] - left, left)
    own, own_low, own_high = pack(spectra, offsets, bins, (shape[0] - left, left))
    near = fetched(own, NEAR)
    far = fetched(own, FAR)
    pair_low = fetched(own_low, PAIR)
    pair_high = fetched(own_high, PAIR)

    query, total = chip_terms(shape, axis, own, pair_low, left)
    terms = functools.partial(band_terms, shape, axis, query)
    own_low, own_high, total = lax.optimization_barrier((own_low, own_high, total))
    cross_low = fetched(own_low, CROSS)
    cross_high = fetched(own_high, CROSS)
    total = terms(total, [pair_high], [PAIR], part=high)
    near, total = lax.optimization_barrier((near, total))
    near_pair = fetched(near, PAIR)
    total = terms(total, [near], [NEAR])
    total = terms(total, [near_pair], [NEAR_OF_PAIR])
    for cross, part in ((cross_low, low), (cross_high, high)):
        cross, total = lax.optimization_barrier((cross, total))
        cross_pair = fetched(cross, PAIR)
        total = terms(total, [cross], [CROSS], part=part)
        total = terms(total, [cross_pair], [CROSS_OF_PAIR], part=part)
    far, total = lax.optimization_barrier((far, total))
    return terms(total, [far], [FAR], last=True)


def solution(mesh):
    (axis,) = mesh.axis_names
    return jax.shard_map(
        functools.partial(local, axis, mesh.shape[axis]),
        mesh=mesh,
        in_specs=(P(None, axis, None), P(axis), P()),
        out_specs=P(None, axis, None),
        check_vma=False,
    )
```

```python
import functools
import math

import jax
import jax.numpy as jnp
from jax import lax
from jax.experimental import pallas as pl
from jax.experimental.pallas import tpu as pltpu
from jax.sharding import PartitionSpec as P

spacing_metres = 8
period_metres = 4096
model_amp = 0.5
vmem = 24 << 20

OWN = (0, 0)
PAIR = (1, -1)
NEAR = (2, -2)
CROSS = (-2, 2)
FAR = (-3, 3)
NEAR_OF_PAIR = (-1, 1)
CROSS_OF_PAIR = (3, -3)


def sine(steps):
    half, quarter = period_metres // 2, period_metres // 4
    turn = jnp.bitwise_and(steps + half, period_metres - 1) - half
    turn = jnp.where(turn > quarter, half - turn, jnp.where(turn < -quarter, -half - turn, turn))
    x = turn.astype(jnp.float32) * (2.0 * math.pi / period_metres)
    square = x * x
    total = jnp.full_like(x, -1.0 / math.factorial(11))
    for order in (9, 7, 5, 3, 1):
        total = total * square + (-1.0) ** (order // 2) / math.factorial(order)
    return total * x


def halves(value):
    high = value.astype(jnp.bfloat16).astype(jnp.float32)
    return high, value - high


def rows_of(freqs):
    return -(-2 * freqs // 8) * 8


def angles(tail_ref, block, freqs, channels):
    rows, width = rows_of(freqs), tail_ref.shape[1]
    row = lax.broadcasted_iota(jnp.int32, (rows, channels), 0)
    tail = tail_ref[...].astype(jnp.float32)
    lines = channels // width
    offsets = jnp.concatenate([tail[i : i + 1] for i in range(lines)], axis=1).astype(jnp.int32)
    factor = jnp.concatenate([tail[-rows:]] * lines, axis=1).astype(jnp.int32)
    channel = lax.broadcasted_iota(jnp.int32, (rows, channels), 1) + block * channels
    return factor * (channel * spacing_metres + offsets), row < freqs


def padded(parts, width):
    rows = jnp.concatenate(parts, axis=0)
    rest = jnp.zeros((width - rows.shape[0], rows.shape[1]), jnp.float32)
    return jnp.concatenate([rows, rest], axis=0)


def key_columns(tail_ref, block, freqs, channels, width):
    angle, is_cos = angles(tail_ref, block, freqs, channels)
    high, low = halves(sine(angle + jnp.where(is_cos, period_metres // 4, 0)))
    return padded([high, low, high, low], width).T.astype(jnp.bfloat16)


def query_rows(tail_ref, block, freqs, channels, width):
    angle, is_cos = angles(tail_ref, block, freqs, channels)
    quarter = period_metres // 4
    high, low = halves(-model_amp * sine(angle + jnp.where(is_cos, quarter, 0)))
    real = padded([high, high, low, low], width)
    high, low = halves(model_amp * sine(angle - jnp.where(is_cos, 0, quarter)))
    imag = padded([high, high, low, low], width)
    return real, imag


def turned(value):
    half = value.shape[0] // 2
    return jnp.concatenate([-value[half:], value[:half]], axis=0)


def block_of(axis, place):
    me = lax.axis_index(axis)
    return me + place[0] + lax.rem(me, 2) * (place[1] - place[0])


def pack_kernel(spectra_ref, off_ref, bins_ref, *refs):
    out_refs, (off, bins, sems) = refs[:-3], refs[-3:]
    width = spectra_ref.shape[1]
    freqs, lines = bins_ref.shape[0], off.shape[1] // width
    tail = (-(-(lines + rows_of(freqs)) // 16) * 16, width)
    sources, targets, start = [off_ref, bins_ref], [off, bins], 0
    for out_ref in out_refs:
        rows = out_ref.shape[0] - tail[0]
        sources.append(spectra_ref.at[pl.ds(start, rows)])
        targets.append(out_ref.at[pl.ds(0, rows)])
        start = (start + rows) % spectra_ref.shape[0]
    copies = [
        pltpu.make_async_copy(source, target, sems.at[i])
        for i, (source, target) in enumerate(zip(sources, targets))
    ]
    for copy in copies:
        copy.start()
    for copy in copies[:2]:
        copy.wait()
    row = lax.broadcasted_iota(jnp.int32, tail, 0)
    value = jnp.zeros(tail, jnp.int32)
    for i in range(lines):
        value = jnp.where(row == i, off[:, i * width : (i + 1) * width], value)
    first = tail[0] - rows_of(freqs)
    for f in range(freqs):
        value = jnp.where((row == first + f) | (row == first + freqs + f), bins[f], value)
    for out_ref in out_refs:
        out_ref[out_ref.shape[0] - tail[0] :, :] = value.astype(jnp.float32).astype(jnp.bfloat16)
    for copy in copies[2:]:
        copy.wait()


def pack(spectra, offsets, bins, parts):
    freqs, channels, width = spectra.shape
    tail = -(-(channels // width + rows_of(freqs)) // 16) * 16
    whole = pl.BlockSpec(memory_space=pltpu.VMEM)
    return pl.pallas_call(
        pack_kernel,
        out_shape=[
            jax.ShapeDtypeStruct((part * channels + tail, width), spectra.dtype)
            for part in (freqs, *parts)
        ],
        in_specs=[pl.BlockSpec(memory_space=pltpu.HBM)] * 3,
        out_specs=[whole] * (1 + len(parts)),
        scratch_shapes=[
            pltpu.VMEM((1, channels), jnp.int32),
            pltpu.SMEM((freqs,), jnp.int32),
            pltpu.SemaphoreType.DMA((3 + len(parts),)),
        ],
        compiler_params=pltpu.CompilerParams(vmem_limit_bytes=vmem),
        cost_estimate=pl.CostEstimate(flops=0, bytes_accessed=1 << 20, transcendentals=0),
    )(
        *(
            pltpu.with_memory_space_constraint(value, pltpu.HBM)
            for value in (spectra.reshape(freqs * channels, width), offsets.reshape(1, channels), bins)
        )
    )


def fill_queries(own_ref, query_ref, block):
    freqs, channels, width = query_ref.shape[0], query_ref.shape[2] // 2, own_ref.shape[1]
    tail_ref = own_ref.at[pl.ds(freqs * channels, own_ref.shape[0] - freqs * channels)]
    real, imag = query_rows(tail_ref, block, freqs, channels, width)
    row = lax.rem(lax.broadcasted_iota(jnp.int32, (width, channels), 0), rows_of(freqs))
    for f in range(freqs):
        own = own_ref[pl.ds(f * channels, channels), :].astype(jnp.float32).T * (2.0 / width)
        mine = (row == f) | (row == freqs + f)
        query_ref[f, :width, :channels] = own.astype(jnp.bfloat16)
        query_ref[f, :width, channels:] = (-turned(own)).astype(jnp.bfloat16)
        query_ref[f, width:, :channels] = jnp.where(mine, real, 0.0).astype(jnp.bfloat16)
        query_ref[f, width:, channels:] = jnp.where(mine, imag, 0.0).astype(jnp.bfloat16)


def band_sums(query_ref, keys, f, extra, first=0):
    channels = query_ref.shape[2] // 2
    spectra = [key_ref[pl.ds((f - first) * channels, channels), :] for key_ref in keys]
    spectra = spectra[0] if len(keys) == 1 else jnp.concatenate(spectra, axis=0)
    extra = extra[0] if len(keys) == 1 else jnp.concatenate(extra, axis=0)
    misfit = jnp.dot(
        jnp.concatenate([spectra, extra], axis=1), query_ref[f], preferred_element_type=jnp.float32
    )
    grad = jnp.tanh(misfit).astype(jnp.bfloat16)
    sums = jnp.dot(spectra.T, grad, preferred_element_type=jnp.float32)
    return sums[:, :channels] + turned(sums[:, channels:])


def columns_of(key_ref, block, freqs, channels, width):
    tail = -(-(channels // width + rows_of(freqs)) // 16) * 16
    tail_ref = key_ref.at[pl.ds(key_ref.shape[0] - tail, tail)]
    return key_columns(tail_ref, block, freqs, channels, width)


def chip_kernel(axis, left, own_ref, pair_ref, query_ref, total_ref):
    freqs, width, channels = total_ref.shape
    own, pair = block_of(axis, OWN), block_of(axis, PAIR)
    fill_queries(own_ref, query_ref, own)
    own_columns = columns_of(own_ref, own, freqs, channels, width)
    pair_columns = columns_of(pair_ref, pair, freqs, channels, width)
    for f in range(freqs):
        term = 2.0 * band_sums(query_ref, [own_ref], f, [own_columns])
        if f < freqs - left:
            term = term + band_sums(query_ref, [pair_ref], f, [pair_columns])
        total_ref[f] = term * (2.0 / width)


def band_kernel(axis, places, first, count, last, query_ref, *refs):
    keys, (total_ref, out_ref) = refs[: len(places)], refs[len(places) : len(places) + 2]
    freqs, width, channels = total_ref.shape
    extra = [
        columns_of(key_ref, block_of(axis, place), freqs, channels, width)
        for key_ref, place in zip(keys, places)
    ]
    copies = []
    for f in range(freqs):
        term = total_ref[f]
        if first <= f < first + count:
            term = term + band_sums(query_ref, keys, f, extra, first) * (2.0 / width)
        if last:
            result_ref, sems = refs[len(places) + 2 :]
            result_ref[f] = term.T
            copies.append(pltpu.make_async_copy(result_ref.at[f], out_ref.at[f], sems.at[f]))
            copies[f].start()
        else:
            out_ref[f] = term
    for copy in copies:
        copy.wait()


def cost(shape, blocks):
    pairs = blocks * shape[0] * shape[1] * shape[1]
    return pl.CostEstimate(
        flops=64 * pairs * shape[2], bytes_accessed=1 << 21, transcendentals=2 * pairs
    )


def chip_terms(shape, axis, own, pair, left):
    freqs, channels, width = shape
    whole = pl.BlockSpec(memory_space=pltpu.VMEM)
    return pl.pallas_call(
        functools.partial(chip_kernel, axis, left),
        out_shape=[
            jax.ShapeDtypeStruct((freqs, 2 * width, 2 * channels), jnp.bfloat16),
            jax.ShapeDtypeStruct((freqs, width, channels), jnp.float32),
        ],
        in_specs=[whole, whole],
        out_specs=[whole, whole],
        compiler_params=pltpu.CompilerParams(vmem_limit_bytes=vmem),
        cost_estimate=cost(shape, 1),
    )(own, pair)


def band_terms(shape, axis, query, total, keys, places, part=None, last=False):
    whole = pl.BlockSpec(memory_space=pltpu.VMEM)
    scratch = [pltpu.VMEM(shape, jnp.float32), pltpu.SemaphoreType.DMA((shape[0],))]
    return pl.pallas_call(
        functools.partial(band_kernel, axis, tuple(places), *(part or (0, shape[0])), last),
        out_shape=jax.ShapeDtypeStruct(shape if last else total.shape, jnp.float32),
        in_specs=[whole] * (len(keys) + 2),
        out_specs=pl.BlockSpec(memory_space=pl.ANY) if last else whole,
        scratch_shapes=scratch if last else [],
        compiler_params=pltpu.CompilerParams(vmem_limit_bytes=vmem),
        cost_estimate=cost(shape, len(keys)),
    )(query, *keys, total)


def local(axis, count, spectra, offsets, bins):
    shape = spectra.shape

    def fetched(value, place):
        sources = [(i + place[i % 2], i) for i in range(count)]
        return lax.ppermute(value, axis, [(i, t) for i, t in sources if 0 <= i < count])

    left = shape[0] // 2
    low, high = (0, shape[0] - left), (shape[0] - left, left)
    own, own_low, own_high = pack(spectra, offsets, bins, (shape[0] - left, left))
    near = fetched(own, NEAR)
    far = fetched(own, FAR)
    pair_low = fetched(own_low, PAIR)
    pair_high = fetched(own_high, PAIR)

    query, total = chip_terms(shape, axis, own, pair_low, left)
    terms = functools.partial(band_terms, shape, axis, query)
    own_low, total = lax.optimization_barrier((own_low, total))
    cross_low = fetched(own_low, CROSS)
    total = terms(total, [pair_high], [PAIR], part=high)
    own_high, total = lax.optimization_barrier((own_high, total))
    cross_high = fetched(own_high, CROSS)
    near, total = lax.optimization_barrier((near, total))
    near_pair = fetched(near, PAIR)
    total = terms(total, [near], [NEAR])
    total = terms(total, [near_pair], [NEAR_OF_PAIR])
    for cross, part in ((cross_low, low), (cross_high, high)):
        cross, total = lax.optimization_barrier((cross, total))
        cross_pair = fetched(cross, PAIR)
        total = terms(total, [cross], [CROSS], part=part)
        total = terms(total, [cross_pair], [CROSS_OF_PAIR], part=part)
    far, total = lax.optimization_barrier((far, total))
    return terms(total, [far], [FAR], last=True)


def solution(mesh):
    (axis,) = mesh.axis_names
    return jax.shard_map(
        functools.partial(local, axis, mesh.shape[axis]),
        mesh=mesh,
        in_specs=(P(None, axis, None), P(axis), P()),
        out_specs=P(None, axis, None),
        check_vma=False,
    )
```

```python
import functools
import math

import jax
import jax.numpy as jnp
from jax import lax
from jax.experimental import pallas as pl
from jax.experimental.pallas import tpu as pltpu
from jax.sharding import PartitionSpec as P

spacing_metres = 8
period_metres = 4096
model_amp = 0.5
vmem = 24 << 20
shares = (24, 8, 96, 2, 64, 64, 192, 2)

OWN = (0, 0)
PAIR = (1, -1)
NEAR = (2, -2)
CROSS = (-2, 2)
FAR = (-3, 3)
NEAR_OF_PAIR = (-1, 1)
CROSS_OF_PAIR = (3, -3)


def sine(steps):
    half, quarter = period_metres // 2, period_metres // 4
    turn = jnp.bitwise_and(steps + half, period_metres - 1) - half
    turn = jnp.where(turn > quarter, half - turn, jnp.where(turn < -quarter, -half - turn, turn))
    x = turn.astype(jnp.float32) * (2.0 * math.pi / period_metres)
    square = x * x
    total = jnp.full_like(x, -1.0 / math.factorial(11))
    for order in (9, 7, 5, 3, 1):
        total = total * square + (-1.0) ** (order // 2) / math.factorial(order)
    return total * x


def halves(value):
    high = value.astype(jnp.bfloat16).astype(jnp.float32)
    return high, value - high


def rows_of(freqs):
    return -(-2 * freqs // 8) * 8


def angles(tail_ref, block, freqs, channels):
    rows, width = rows_of(freqs), tail_ref.shape[1]
    row = lax.broadcasted_iota(jnp.int32, (rows, channels), 0)
    tail = tail_ref[...].astype(jnp.float32)
    lines = channels // width
    offsets = jnp.concatenate([tail[i : i + 1] for i in range(lines)], axis=1).astype(jnp.int32)
    factor = jnp.concatenate([tail[-rows:]] * lines, axis=1).astype(jnp.int32)
    channel = lax.broadcasted_iota(jnp.int32, (rows, channels), 1) + block * channels
    return factor * (channel * spacing_metres + offsets), row < freqs


def padded(parts, width):
    rows = jnp.concatenate(parts, axis=0)
    rest = jnp.zeros((width - rows.shape[0], rows.shape[1]), jnp.float32)
    return jnp.concatenate([rows, rest], axis=0)


def key_columns(tail_ref, block, freqs, channels, width):
    angle, is_cos = angles(tail_ref, block, freqs, channels)
    high, low = halves(sine(angle + jnp.where(is_cos, period_metres // 4, 0)))
    return padded([high, low, high, low], width).T.astype(jnp.bfloat16)


def query_rows(tail_ref, block, freqs, channels, width):
    angle, is_cos = angles(tail_ref, block, freqs, channels)
    quarter = period_metres // 4
    high, low = halves(-model_amp * sine(angle + jnp.where(is_cos, quarter, 0)))
    real = padded([high, high, low, low], width)
    high, low = halves(model_amp * sine(angle - jnp.where(is_cos, 0, quarter)))
    imag = padded([high, high, low, low], width)
    return real, imag


def turned(value):
    half = value.shape[0] // 2
    return jnp.concatenate([-value[half:], value[:half]], axis=0)


def block_of(axis, place):
    me = lax.axis_index(axis)
    return me + place[0] + lax.rem(me, 2) * (place[1] - place[0])


def pack_kernel(spectra_ref, off_ref, bins_ref, *refs):
    out_refs, (off, bins, sems) = refs[:-3], refs[-3:]
    width = spectra_ref.shape[1]
    freqs, lines = bins_ref.shape[0], off.shape[1] // width
    tail = (-(-(lines + rows_of(freqs)) // 16) * 16, width)
    sources, targets, start = [off_ref, bins_ref], [off, bins], 0
    for out_ref in out_refs:
        rows = out_ref.shape[0] - tail[0]
        sources.append(spectra_ref.at[pl.ds(start, rows)])
        targets.append(out_ref.at[pl.ds(0, rows)])
        start = (start + rows) % spectra_ref.shape[0]
    copies = [
        pltpu.make_async_copy(source, target, sems.at[i])
        for i, (source, target) in enumerate(zip(sources, targets))
    ]
    for copy in copies:
        copy.start()
    for copy in copies[:2]:
        copy.wait()
    row = lax.broadcasted_iota(jnp.int32, tail, 0)
    value = jnp.zeros(tail, jnp.int32)
    for i in range(lines):
        value = jnp.where(row == i, off[:, i * width : (i + 1) * width], value)
    first = tail[0] - rows_of(freqs)
    for f in range(freqs):
        value = jnp.where((row == first + f) | (row == first + freqs + f), bins[f], value)
    for out_ref in out_refs:
        out_ref[out_ref.shape[0] - tail[0] :, :] = value.astype(jnp.float32).astype(jnp.bfloat16)
    for copy in copies[2:]:
        copy.wait()


def pack(spectra, offsets, bins, parts):
    freqs, channels, width = spectra.shape
    tail = -(-(channels // width + rows_of(freqs)) // 16) * 16
    whole = pl.BlockSpec(memory_space=pltpu.VMEM)
    return pl.pallas_call(
        pack_kernel,
        out_shape=[
            jax.ShapeDtypeStruct((part * channels + tail, width), spectra.dtype)
            for part in (freqs, *parts)
        ],
        in_specs=[pl.BlockSpec(memory_space=pltpu.HBM)] * 3,
        out_specs=[whole] * (1 + len(parts)),
        scratch_shapes=[
            pltpu.VMEM((1, channels), jnp.int32),
            pltpu.SMEM((freqs,), jnp.int32),
            pltpu.SemaphoreType.DMA((3 + len(parts),)),
        ],
        compiler_params=pltpu.CompilerParams(vmem_limit_bytes=vmem),
        cost_estimate=pl.CostEstimate(flops=0, bytes_accessed=1 << 20, transcendentals=0),
    )(
        *(
            pltpu.with_memory_space_constraint(value, pltpu.HBM)
            for value in (spectra.reshape(freqs * channels, width), offsets.reshape(1, channels), bins)
        )
    )


def fill_queries(own_ref, query_ref, block):
    freqs, channels, width = query_ref.shape[0], query_ref.shape[2] // 2, own_ref.shape[1]
    tail_ref = own_ref.at[pl.ds(freqs * channels, own_ref.shape[0] - freqs * channels)]
    real, imag = query_rows(tail_ref, block, freqs, channels, width)
    row = lax.rem(lax.broadcasted_iota(jnp.int32, (width, channels), 0), rows_of(freqs))
    for f in range(freqs):
        own = own_ref[pl.ds(f * channels, channels), :].astype(jnp.float32).T * (2.0 / width)
        mine = (row == f) | (row == freqs + f)
        query_ref[f, :width, :channels] = own.astype(jnp.bfloat16)
        query_ref[f, :width, channels:] = (-turned(own)).astype(jnp.bfloat16)
        query_ref[f, width:, :channels] = jnp.where(mine, real, 0.0).astype(jnp.bfloat16)
        query_ref[f, width:, channels:] = jnp.where(mine, imag, 0.0).astype(jnp.bfloat16)


def band_sums(query_ref, f, keys):
    channels = query_ref.shape[2] // 2
    spectra = [ref[pl.ds((f - first) * channels, channels), :] for ref, first, _ in keys]
    spectra = spectra[0] if len(keys) == 1 else jnp.concatenate(spectra, axis=0)
    extra = [columns for _, _, columns in keys]
    extra = extra[0] if len(keys) == 1 else jnp.concatenate(extra, axis=0)
    misfit = jnp.dot(
        jnp.concatenate([spectra, extra], axis=1), query_ref[f], preferred_element_type=jnp.float32
    )
    grad = jnp.tanh(misfit).astype(jnp.bfloat16)
    sums = jnp.dot(spectra.T, grad, preferred_element_type=jnp.float32)
    return sums[:, :channels] + turned(sums[:, channels:])


def columns_of(key_ref, block, freqs, channels, width):
    tail = -(-(channels // width + rows_of(freqs)) // 16) * 16
    tail_ref = key_ref.at[pl.ds(key_ref.shape[0] - tail, tail)]
    return key_columns(tail_ref, block, freqs, channels, width)


def chip_kernel(axis, low, own_ref, pair_ref, query_ref, total_ref):
    freqs, width, channels = total_ref.shape
    own, pair = block_of(axis, OWN), block_of(axis, PAIR)
    fill_queries(own_ref, query_ref, own)
    own_columns = columns_of(own_ref, own, freqs, channels, width)
    pair_columns = columns_of(pair_ref, pair, freqs, channels, width)
    for f in range(freqs):
        term = 2.0 * band_sums(query_ref, f, [(own_ref, 0, own_columns)])
        if f < low:
            term = term + band_sums(query_ref, f, [(pair_ref, 0, pair_columns)])
        total_ref[f] = term * (2.0 / width)


def holds(span, f):
    return span[0] <= f < span[0] + span[1]


def band_kernel(axis, places, spans, held, span, last, query_ref, *refs):
    keys, refs = refs[: len(places)], refs[len(places) :]
    total_refs, out_refs = refs[: len(held)], refs[len(held) :]
    freqs = query_ref.shape[0]
    _, width, channels = total_refs[0].shape
    extra = [
        columns_of(key_ref, block_of(axis, place), freqs, channels, width)
        for key_ref, place in zip(keys, places)
    ]
    copies = []
    for f in range(span[0], span[0] + span[1]):
        used = [
            (key_ref, part[0], columns)
            for key_ref, part, columns in zip(keys, spans, extra)
            if holds(part, f)
        ]
        total = next(ref[f - part[0]] for ref, part in zip(total_refs, held) if holds(part, f))
        term = total + band_sums(query_ref, f, used) * (2.0 / width)
        if last:
            out_ref, result_ref, sems = out_refs
            result_ref[f] = term.T
            copies.append(pltpu.make_async_copy(result_ref.at[f], out_ref.at[f], sems.at[f]))
            copies[-1].start()
        else:
            out_refs[0][f - span[0]] = term
    for copy in copies:
        copy.wait()


def cost(shape, share):
    pairs = shape[0] * shape[1] * shape[1]
    return pl.CostEstimate(
        flops=share * pairs * shape[2], bytes_accessed=1 << 21, transcendentals=2 * pairs
    )


def chip_terms(shape, axis, low, own, pair, share):
    freqs, channels, width = shape
    whole = pl.BlockSpec(memory_space=pltpu.VMEM)
    return pl.pallas_call(
        functools.partial(chip_kernel, axis, low),
        out_shape=[
            jax.ShapeDtypeStruct((freqs, 2 * width, 2 * channels), jnp.bfloat16),
            jax.ShapeDtypeStruct((freqs, width, channels), jnp.float32),
        ],
        in_specs=[whole, whole],
        out_specs=[whole, whole],
        compiler_params=pltpu.CompilerParams(vmem_limit_bytes=vmem),
        cost_estimate=cost(shape, share),
    )(own, pair)


def band_terms(shape, axis, query, totals, keys, span, share, last=False):
    freqs, channels, width = shape
    whole = pl.BlockSpec(memory_space=pltpu.VMEM)
    out = shape if last else (span[1], width, channels)
    scratch = [pltpu.VMEM(shape, jnp.float32), pltpu.SemaphoreType.DMA((freqs,))]
    places, spans = tuple(key[1] for key in keys), tuple(key[2] for key in keys)
    held = tuple(total[1] for total in totals)
    return pl.pallas_call(
        functools.partial(band_kernel, axis, places, spans, held, span, last),
        out_shape=jax.ShapeDtypeStruct(out, jnp.float32),
        in_specs=[whole] * (1 + len(keys) + len(totals)),
        out_specs=pl.BlockSpec(memory_space=pl.ANY) if last else whole,
        scratch_shapes=scratch if last else [],
        compiler_params=pltpu.CompilerParams(vmem_limit_bytes=vmem),
        cost_estimate=cost(shape, share),
    )(query, *(key[0] for key in keys), *(total[0] for total in totals))


def local(axis, count, spectra, offsets, bins):
    shape = spectra.shape

    def fetched(value, place):
        sources = [(i + place[i % 2], i) for i in range(count)]
        return lax.ppermute(value, axis, [(i, t) for i, t in sources if 0 <= i < count])

    left = shape[0] // 2
    every, low, high = (0, shape[0]), (0, shape[0] - left), (shape[0] - left, left)
    own, own_low, own_high = pack(spectra, offsets, bins, (low[1], high[1]))
    near = fetched(own, NEAR)
    far = fetched(own, FAR)
    pair_low = fetched(own_low, PAIR)
    pair_high = fetched(own_high, PAIR)

    query, total = chip_terms(shape, axis, low[1], own, pair_low, shares[0])
    terms = functools.partial(band_terms, shape, axis, query)
    own_low, total = lax.optimization_barrier((own_low, total))
    cross_low = fetched(own_low, CROSS)
    rest = terms([(total, every)], [(pair_high, PAIR, high)], high, shares[1])
    own_high, rest = lax.optimization_barrier((own_high, rest))
    cross_high = fetched(own_high, CROSS)
    near, rest = lax.optimization_barrier((near, rest))
    near_pair = fetched(near, PAIR)
    total = terms([(rest, high), (total, every)], [(near, NEAR, every)], every, shares[2])
    total = terms([(total, every)], [(near_pair, NEAR_OF_PAIR, every)], every, shares[3])
    cross_high, total = lax.optimization_barrier((cross_high, total))
    high_pair = fetched(cross_high, PAIR)
    rest = terms([(total, every)], [(cross_high, CROSS, high)], high, shares[4])
    rest = terms([(rest, high)], [(high_pair, CROSS_OF_PAIR, high)], high, shares[5])
    cross_low, rest = lax.optimization_barrier((cross_low, rest))
    low_pair = fetched(cross_low, PAIR)
    first = terms([(total, every)], [(cross_low, CROSS, low)], low, shares[6])
    far, first = lax.optimization_barrier((far, first))
    closing = [(low_pair, CROSS_OF_PAIR, low), (far, FAR, every)]
    return terms([(first, low), (rest, high)], closing, every, shares[7], last=True)


def solution(mesh):
    (axis,) = mesh.axis_names
    return jax.shard_map(
        functools.partial(local, axis, mesh.shape[axis]),
        mesh=mesh,
        in_specs=(P(None, axis, None), P(axis), P()),
        out_specs=P(None, axis, None),
        check_vma=False,
    )
```

```python
import functools
import math

import jax
import jax.numpy as jnp
from jax import lax
from jax.experimental import pallas as pl
from jax.experimental.pallas import tpu as pltpu
from jax.sharding import PartitionSpec as P

spacing_metres = 8
period_metres = 4096
model_amp = 0.5
vmem = 24 << 20
shares = (24, 8, 96, 2, 64, 64, 192, 2)

OWN = (0, 0, 0, 0)
PAIR = (1, -1, 1, -1)
NEAR = (2, 2, -2, -2)
CROSS = (-2, -2, 2, 2)
FAR = (-3, 3, -3, 3)
NEAR_OF_PAIR = (3, 1, -1, -3)
CROSS_OF_PAIR = (-1, -3, 3, 1)


def sine(steps):
    half, quarter = period_metres // 2, period_metres // 4
    turn = jnp.bitwise_and(steps + half, period_metres - 1) - half
    turn = jnp.where(turn > quarter, half - turn, jnp.where(turn < -quarter, -half - turn, turn))
    x = turn.astype(jnp.float32) * (2.0 * math.pi / period_metres)
    square = x * x
    total = jnp.full_like(x, -1.0 / math.factorial(11))
    for order in (9, 7, 5, 3, 1):
        total = total * square + (-1.0) ** (order // 2) / math.factorial(order)
    return total * x


def halves(value):
    high = value.astype(jnp.bfloat16).astype(jnp.float32)
    return high, value - high


def rows_of(freqs):
    return -(-2 * freqs // 8) * 8


def angles(tail_ref, block, freqs, channels):
    rows, width = rows_of(freqs), tail_ref.shape[1]
    row = lax.broadcasted_iota(jnp.int32, (rows, channels), 0)
    tail = tail_ref[...].astype(jnp.float32)
    lines = channels // width
    offsets = jnp.concatenate([tail[i : i + 1] for i in range(lines)], axis=1).astype(jnp.int32)
    factor = jnp.concatenate([tail[-rows:]] * lines, axis=1).astype(jnp.int32)
    channel = lax.broadcasted_iota(jnp.int32, (rows, channels), 1) + block * channels
    return factor * (channel * spacing_metres + offsets), row < freqs


def padded(parts, width):
    rows = jnp.concatenate(parts, axis=0)
    rest = jnp.zeros((width - rows.shape[0], rows.shape[1]), jnp.float32)
    return jnp.concatenate([rows, rest], axis=0)


def key_columns(tail_ref, block, freqs, channels, width):
    angle, is_cos = angles(tail_ref, block, freqs, channels)
    high, low = halves(sine(angle + jnp.where(is_cos, period_metres // 4, 0)))
    return padded([high, low, high, low], width).T.astype(jnp.bfloat16)


def query_rows(tail_ref, block, freqs, channels, width):
    angle, is_cos = angles(tail_ref, block, freqs, channels)
    quarter = period_metres // 4
    high, low = halves(-model_amp * sine(angle + jnp.where(is_cos, quarter, 0)))
    real = padded([high, high, low, low], width)
    high, low = halves(model_amp * sine(angle - jnp.where(is_cos, 0, quarter)))
    imag = padded([high, high, low, low], width)
    return real, imag


def turned(value):
    half = value.shape[0] // 2
    return jnp.concatenate([-value[half:], value[:half]], axis=0)


def block_of(axis, place):
    me = lax.axis_index(axis)
    kind = lax.rem(me, len(place))
    step = place[0]
    for i in range(1, len(place)):
        step = jnp.where(kind == i, place[i], step)
    return me + step


def pack_kernel(spectra_ref, off_ref, bins_ref, *refs):
    out_refs, (off, bins, sems) = refs[:-3], refs[-3:]
    width = spectra_ref.shape[1]
    freqs, lines = bins_ref.shape[0], off.shape[1] // width
    tail = (-(-(lines + rows_of(freqs)) // 16) * 16, width)
    sources, targets, start = [off_ref, bins_ref], [off, bins], 0
    for out_ref in out_refs:
        rows = out_ref.shape[0] - tail[0]
        sources.append(spectra_ref.at[pl.ds(start, rows)])
        targets.append(out_ref.at[pl.ds(0, rows)])
        start = (start + rows) % spectra_ref.shape[0]
    copies = [
        pltpu.make_async_copy(source, target, sems.at[i])
        for i, (source, target) in enumerate(zip(sources, targets))
    ]
    for copy in copies:
        copy.start()
    for copy in copies[:2]:
        copy.wait()
    row = lax.broadcasted_iota(jnp.int32, tail, 0)
    value = jnp.zeros(tail, jnp.int32)
    for i in range(lines):
        value = jnp.where(row == i, off[:, i * width : (i + 1) * width], value)
    first = tail[0] - rows_of(freqs)
    for f in range(freqs):
        value = jnp.where((row == first + f) | (row == first + freqs + f), bins[f], value)
    for out_ref in out_refs:
        out_ref[out_ref.shape[0] - tail[0] :, :] = value.astype(jnp.float32).astype(jnp.bfloat16)
    for copy in copies[2:]:
        copy.wait()


def pack(spectra, offsets, bins, parts):
    freqs, channels, width = spectra.shape
    tail = -(-(channels // width + rows_of(freqs)) // 16) * 16
    whole = pl.BlockSpec(memory_space=pltpu.VMEM)
    return pl.pallas_call(
        pack_kernel,
        out_shape=[
            jax.ShapeDtypeStruct((part * channels + tail, width), spectra.dtype)
            for part in (freqs, *parts)
        ],
        in_specs=[pl.BlockSpec(memory_space=pltpu.HBM)] * 3,
        out_specs=[whole] * (1 + len(parts)),
        scratch_shapes=[
            pltpu.VMEM((1, channels), jnp.int32),
            pltpu.SMEM((freqs,), jnp.int32),
            pltpu.SemaphoreType.DMA((3 + len(parts),)),
        ],
        compiler_params=pltpu.CompilerParams(vmem_limit_bytes=vmem),
        cost_estimate=pl.CostEstimate(flops=0, bytes_accessed=1 << 20, transcendentals=0),
    )(
        *(
            pltpu.with_memory_space_constraint(value, pltpu.HBM)
            for value in (spectra.reshape(freqs * channels, width), offsets.reshape(1, channels), bins)
        )
    )


def fill_queries(own_ref, query_ref, block):
    freqs, channels, width = query_ref.shape[0], query_ref.shape[2] // 2, own_ref.shape[1]
    tail_ref = own_ref.at[pl.ds(freqs * channels, own_ref.shape[0] - freqs * channels)]
    real, imag = query_rows(tail_ref, block, freqs, channels, width)
    row = lax.rem(lax.broadcasted_iota(jnp.int32, (width, channels), 0), rows_of(freqs))
    for f in range(freqs):
        own = own_ref[pl.ds(f * channels, channels), :].astype(jnp.float32).T * (2.0 / width)
        mine = (row == f) | (row == freqs + f)
        query_ref[f, :width, :channels] = own.astype(jnp.bfloat16)
        query_ref[f, :width, channels:] = (-turned(own)).astype(jnp.bfloat16)
        query_ref[f, width:, :channels] = jnp.where(mine, real, 0.0).astype(jnp.bfloat16)
        query_ref[f, width:, channels:] = jnp.where(mine, imag, 0.0).astype(jnp.bfloat16)


def band_sums(query_ref, f, keys):
    channels = query_ref.shape[2] // 2
    spectra = [ref[pl.ds((f - first) * channels, channels), :] for ref, first, _ in keys]
    spectra = spectra[0] if len(keys) == 1 else jnp.concatenate(spectra, axis=0)
    extra = [columns for _, _, columns in keys]
    extra = extra[0] if len(keys) == 1 else jnp.concatenate(extra, axis=0)
    misfit = jnp.dot(
        jnp.concatenate([spectra, extra], axis=1), query_ref[f], preferred_element_type=jnp.float32
    )
    grad = jnp.tanh(misfit).astype(jnp.bfloat16)
    sums = jnp.dot(spectra.T, grad, preferred_element_type=jnp.float32)
    return sums[:, :channels] + turned(sums[:, channels:])


def columns_of(key_ref, block, freqs, channels, width):
    tail = -(-(channels // width + rows_of(freqs)) // 16) * 16
    tail_ref = key_ref.at[pl.ds(key_ref.shape[0] - tail, tail)]
    return key_columns(tail_ref, block, freqs, channels, width)


def chip_kernel(axis, low, own_ref, pair_ref, query_ref, total_ref):
    freqs, width, channels = total_ref.shape
    own, pair = block_of(axis, OWN), block_of(axis, PAIR)
    fill_queries(own_ref, query_ref, own)
    own_columns = columns_of(own_ref, own, freqs, channels, width)
    pair_columns = columns_of(pair_ref, pair, freqs, channels, width)
    for f in range(freqs):
        term = 2.0 * band_sums(query_ref, f, [(own_ref, 0, own_columns)])
        if f < low:
            term = term + band_sums(query_ref, f, [(pair_ref, 0, pair_columns)])
        total_ref[f] = term * (2.0 / width)


def holds(span, f):
    return span[0] <= f < span[0] + span[1]


def band_kernel(axis, places, spans, held, span, last, query_ref, *refs):
    keys, refs = refs[: len(places)], refs[len(places) :]
    total_refs, out_refs = refs[: len(held)], refs[len(held) :]
    freqs = query_ref.shape[0]
    _, width, channels = total_refs[0].shape
    extra = [
        columns_of(key_ref, block_of(axis, place), freqs, channels, width)
        for key_ref, place in zip(keys, places)
    ]
    copies = []
    for f in range(span[0], span[0] + span[1]):
        used = [
            (key_ref, part[0], columns)
            for key_ref, part, columns in zip(keys, spans, extra)
            if holds(part, f)
        ]
        total = next(ref[f - part[0]] for ref, part in zip(total_refs, held) if holds(part, f))
        term = total + band_sums(query_ref, f, used) * (2.0 / width) if used else total
        if last:
            out_ref, result_ref, sems = out_refs
            result_ref[f] = term.T
            copies.append(pltpu.make_async_copy(result_ref.at[f], out_ref.at[f], sems.at[f]))
            copies[-1].start()
        else:
            out_refs[0][f - span[0]] = term
    for copy in copies:
        copy.wait()


def cost(shape, share):
    pairs = shape[0] * shape[1] * shape[1]
    return pl.CostEstimate(
        flops=share * pairs * shape[2], bytes_accessed=1 << 21, transcendentals=2 * pairs
    )


def chip_terms(shape, axis, low, own, pair, share):
    freqs, channels, width = shape
    whole = pl.BlockSpec(memory_space=pltpu.VMEM)
    return pl.pallas_call(
        functools.partial(chip_kernel, axis, low),
        out_shape=[
            jax.ShapeDtypeStruct((freqs, 2 * width, 2 * channels), jnp.bfloat16),
            jax.ShapeDtypeStruct((freqs, width, channels), jnp.float32),
        ],
        in_specs=[whole, whole],
        out_specs=[whole, whole],
        compiler_params=pltpu.CompilerParams(vmem_limit_bytes=vmem),
        cost_estimate=cost(shape, share),
    )(own, pair)


def band_terms(shape, axis, query, totals, keys, span, share, last=False):
    freqs, channels, width = shape
    whole = pl.BlockSpec(memory_space=pltpu.VMEM)
    out = shape if last else (span[1], width, channels)
    scratch = [pltpu.VMEM(shape, jnp.float32), pltpu.SemaphoreType.DMA((freqs,))]
    places, spans = tuple(key[1] for key in keys), tuple(key[2] for key in keys)
    held = tuple(total[1] for total in totals)
    return pl.pallas_call(
        functools.partial(band_kernel, axis, places, spans, held, span, last),
        out_shape=jax.ShapeDtypeStruct(out, jnp.float32),
        in_specs=[whole] * (1 + len(keys) + len(totals)),
        out_specs=pl.BlockSpec(memory_space=pl.ANY) if last else whole,
        scratch_shapes=scratch if last else [],
        compiler_params=pltpu.CompilerParams(vmem_limit_bytes=vmem),
        cost_estimate=cost(shape, share),
    )(query, *(key[0] for key in keys), *(total[0] for total in totals))


def local(axis, count, spectra, offsets, bins):
    shape = spectra.shape

    def fetched(value, place):
        sources = [(i + place[i % len(place)], i) for i in range(count)]
        return lax.ppermute(value, axis, [(i, t) for i, t in sources if 0 <= i < count])

    left = shape[0] // 2
    every, low, high = (0, shape[0]), (0, shape[0] - left), (shape[0] - left, left)
    own, own_low, own_high = pack(spectra, offsets, bins, (low[1], high[1]))
    near = fetched(own, NEAR)
    far = fetched(own, FAR)
    pair_low = fetched(own_low, PAIR)
    pair_high = fetched(own_high, PAIR)

    query, total = chip_terms(shape, axis, low[1], own, pair_low, shares[0])
    terms = functools.partial(band_terms, shape, axis, query)
    own_low, total = lax.optimization_barrier((own_low, total))
    cross_low = fetched(own_low, CROSS)
    rest = terms([(total, every)], [(pair_high, PAIR, high)], high, shares[1])
    own_high, rest = lax.optimization_barrier((own_high, rest))
    cross_high = fetched(own_high, CROSS)
    near, rest = lax.optimization_barrier((near, rest))
    near_pair = fetched(near, PAIR)
    total = terms([(rest, high), (total, every)], [(near, NEAR, every)], every, shares[2])
    total = terms([(total, every)], [(near_pair, NEAR_OF_PAIR, every)], every, shares[3])
    cross_high, total = lax.optimization_barrier((cross_high, total))
    high_pair = fetched(cross_high, PAIR)
    rest = terms([(total, every)], [(cross_high, CROSS, high)], high, shares[4])
    rest = terms([(rest, high)], [(high_pair, CROSS_OF_PAIR, high)], high, shares[5])
    cross_low, rest = lax.optimization_barrier((cross_low, rest))
    low_pair = fetched(cross_low, PAIR)
    first = terms([(total, every)], [(cross_low, CROSS, low)], low, shares[6])
    far, first = lax.optimization_barrier((far, first))
    closing = [(low_pair, CROSS_OF_PAIR, low), (far, FAR, every)]
    return terms([(first, low), (rest, high)], closing, every, shares[7], last=True)


def solution(mesh):
    (axis,) = mesh.axis_names
    return jax.shard_map(
        functools.partial(local, axis, mesh.shape[axis]),
        mesh=mesh,
        in_specs=(P(None, axis, None), P(axis), P()),
        out_specs=P(None, axis, None),
        check_vma=False,
    )
```

```python
import functools
import math

import jax
import jax.numpy as jnp
from jax import lax
from jax.experimental import pallas as pl
from jax.experimental.pallas import tpu as pltpu
from jax.sharding import PartitionSpec as P

spacing_metres = 8
period_metres = 4096
model_amp = 0.5
vmem = 24 << 20
shares = (64, 64, 64, 64, 64, 64, 64, 64, 64)

OWN = (0, 0, 0, 0)
PAIR = (1, -1, 1, -1)
NEAR = (2, 2, -2, -2)
CROSS = (-2, -2, 2, 2)
FAR = (-3, 3, -3, 3)
NEAR_OF_PAIR = (3, 1, -1, -3)
CROSS_OF_PAIR = (-1, -3, 3, 1)


def sine(steps):
    half, quarter = period_metres // 2, period_metres // 4
    turn = jnp.bitwise_and(steps + half, period_metres - 1) - half
    turn = jnp.where(turn > quarter, half - turn, jnp.where(turn < -quarter, -half - turn, turn))
    x = turn.astype(jnp.float32) * (2.0 * math.pi / period_metres)
    square = x * x
    total = jnp.full_like(x, -1.0 / math.factorial(11))
    for order in (9, 7, 5, 3, 1):
        total = total * square + (-1.0) ** (order // 2) / math.factorial(order)
    return total * x


def halves(value):
    high = value.astype(jnp.bfloat16).astype(jnp.float32)
    return high, value - high


def rows_of(freqs):
    return -(-2 * freqs // 8) * 8


def angles(tail_ref, block, freqs, channels):
    rows, width = rows_of(freqs), tail_ref.shape[1]
    row = lax.broadcasted_iota(jnp.int32, (rows, channels), 0)
    tail = tail_ref[...].astype(jnp.float32)
    lines = channels // width
    offsets = jnp.concatenate([tail[i : i + 1] for i in range(lines)], axis=1).astype(jnp.int32)
    factor = jnp.concatenate([tail[-rows:]] * lines, axis=1).astype(jnp.int32)
    channel = lax.broadcasted_iota(jnp.int32, (rows, channels), 1) + block * channels
    return factor * (channel * spacing_metres + offsets), row < freqs


def padded(parts, width):
    rows = jnp.concatenate(parts, axis=0)
    rest = jnp.zeros((width - rows.shape[0], rows.shape[1]), jnp.float32)
    return jnp.concatenate([rows, rest], axis=0)


def key_columns(tail_ref, block, freqs, channels, width):
    angle, is_cos = angles(tail_ref, block, freqs, channels)
    high, low = halves(sine(angle + jnp.where(is_cos, period_metres // 4, 0)))
    return padded([high, low, high, low], width).T.astype(jnp.bfloat16)


def query_rows(tail_ref, block, freqs, channels, width):
    angle, is_cos = angles(tail_ref, block, freqs, channels)
    quarter = period_metres // 4
    high, low = halves(-model_amp * sine(angle + jnp.where(is_cos, quarter, 0)))
    real = padded([high, high, low, low], width)
    high, low = halves(model_amp * sine(angle - jnp.where(is_cos, 0, quarter)))
    imag = padded([high, high, low, low], width)
    return real, imag


def turned(value):
    half = value.shape[0] // 2
    return jnp.concatenate([-value[half:], value[:half]], axis=0)


def block_of(axis, place):
    me = lax.axis_index(axis)
    kind = lax.rem(me, len(place))
    step = place[0]
    for i in range(1, len(place)):
        step = jnp.where(kind == i, place[i], step)
    return me + step


def pack_kernel(spectra_ref, off_ref, bins_ref, *refs):
    out_refs, (off, bins, sems) = refs[:-3], refs[-3:]
    width = spectra_ref.shape[1]
    freqs, lines = bins_ref.shape[0], off.shape[1] // width
    tail = (-(-(lines + rows_of(freqs)) // 16) * 16, width)
    sources, targets, start = [off_ref, bins_ref], [off, bins], 0
    for out_ref in out_refs:
        rows = out_ref.shape[0] - tail[0]
        sources.append(spectra_ref.at[pl.ds(start, rows)])
        targets.append(out_ref.at[pl.ds(0, rows)])
        start = (start + rows) % spectra_ref.shape[0]
    copies = [
        pltpu.make_async_copy(source, target, sems.at[i])
        for i, (source, target) in enumerate(zip(sources, targets))
    ]
    for copy in copies:
        copy.start()
    for copy in copies[:2]:
        copy.wait()
    row = lax.broadcasted_iota(jnp.int32, tail, 0)
    value = jnp.zeros(tail, jnp.int32)
    for i in range(lines):
        value = jnp.where(row == i, off[:, i * width : (i + 1) * width], value)
    first = tail[0] - rows_of(freqs)
    for f in range(freqs):
        value = jnp.where((row == first + f) | (row == first + freqs + f), bins[f], value)
    for out_ref in out_refs:
        out_ref[out_ref.shape[0] - tail[0] :, :] = value.astype(jnp.float32).astype(jnp.bfloat16)
    for copy in copies[2:]:
        copy.wait()


def pack(spectra, offsets, bins, parts):
    freqs, channels, width = spectra.shape
    tail = -(-(channels // width + rows_of(freqs)) // 16) * 16
    whole = pl.BlockSpec(memory_space=pltpu.VMEM)
    return pl.pallas_call(
        pack_kernel,
        out_shape=[
            jax.ShapeDtypeStruct((part * channels + tail, width), spectra.dtype)
            for part in (freqs, *parts)
        ],
        in_specs=[pl.BlockSpec(memory_space=pltpu.HBM)] * 3,
        out_specs=[whole] * (1 + len(parts)),
        scratch_shapes=[
            pltpu.VMEM((1, channels), jnp.int32),
            pltpu.SMEM((freqs,), jnp.int32),
            pltpu.SemaphoreType.DMA((3 + len(parts),)),
        ],
        compiler_params=pltpu.CompilerParams(vmem_limit_bytes=vmem),
        cost_estimate=pl.CostEstimate(flops=0, bytes_accessed=1 << 20, transcendentals=0),
    )(
        *(
            pltpu.with_memory_space_constraint(value, pltpu.HBM)
            for value in (spectra.reshape(freqs * channels, width), offsets.reshape(1, channels), bins)
        )
    )


def fill_queries(own_ref, query_ref, block):
    freqs, channels, width = query_ref.shape[0], query_ref.shape[2] // 2, own_ref.shape[1]
    tail_ref = own_ref.at[pl.ds(freqs * channels, own_ref.shape[0] - freqs * channels)]
    real, imag = query_rows(tail_ref, block, freqs, channels, width)
    row = lax.rem(lax.broadcasted_iota(jnp.int32, (width, channels), 0), rows_of(freqs))
    for f in range(freqs):
        own = own_ref[pl.ds(f * channels, channels), :].astype(jnp.float32).T * (2.0 / width)
        mine = (row == f) | (row == freqs + f)
        query_ref[f, :width, :channels] = own.astype(jnp.bfloat16)
        query_ref[f, :width, channels:] = (-turned(own)).astype(jnp.bfloat16)
        query_ref[f, width:, :channels] = jnp.where(mine, real, 0.0).astype(jnp.bfloat16)
        query_ref[f, width:, channels:] = jnp.where(mine, imag, 0.0).astype(jnp.bfloat16)


def spectra_of(f, keys):
    parts = []
    for ref, first, _ in keys:
        channels = keys[0][2].shape[0]
        parts.append(ref[pl.ds((f - first) * channels, channels), :])
    return parts[0] if len(parts) == 1 else jnp.concatenate(parts, axis=0)


def misfit_of(query_ref, f, keys):
    extra = [columns for _, _, columns in keys]
    extra = extra[0] if len(keys) == 1 else jnp.concatenate(extra, axis=0)
    key = jnp.concatenate([spectra_of(f, keys), extra], axis=1)
    return jnp.dot(key, query_ref[f], preferred_element_type=jnp.float32)


def band_sums(query_ref, steps, emit):
    channels = query_ref.shape[2] // 2
    ahead = misfit_of(query_ref, *steps[0])
    for i, (f, keys) in enumerate(steps):
        misfit = ahead
        if i + 1 < len(steps):
            ahead = misfit_of(query_ref, *steps[i + 1])
        grad = jnp.tanh(misfit).astype(jnp.bfloat16)
        sums = jnp.dot(spectra_of(f, keys).T, grad, preferred_element_type=jnp.float32)
        emit(i, f, sums[:, :channels] + turned(sums[:, channels:]))


def columns_of(key_ref, block, freqs, channels, width):
    tail = -(-(channels // width + rows_of(freqs)) // 16) * 16
    tail_ref = key_ref.at[pl.ds(key_ref.shape[0] - tail, tail)]
    return key_columns(tail_ref, block, freqs, channels, width)


def chip_kernel(axis, low, own_ref, pair_ref, query_ref, total_ref):
    freqs, width, channels = total_ref.shape
    own, pair = block_of(axis, OWN), block_of(axis, PAIR)
    fill_queries(own_ref, query_ref, own)
    own_columns = columns_of(own_ref, own, freqs, channels, width)
    pair_columns = columns_of(pair_ref, pair, freqs, channels, width)
    steps = []
    for f in range(freqs):
        steps.append((f, [(own_ref, 0, own_columns)]))
        if f < low:
            steps.append((f, [(pair_ref, 0, pair_columns)]))

    def emit(i, f, sums):
        if steps[i][1][0][0] is own_ref:
            total_ref[f] = sums * (4.0 / width)
        else:
            total_ref[f] += sums * (2.0 / width)

    band_sums(query_ref, steps, emit)


def holds(span, f):
    return span[0] <= f < span[0] + span[1]


def band_kernel(axis, places, spans, held, span, last, query_ref, *refs):
    keys, refs = refs[: len(places)], refs[len(places) :]
    total_refs, out_refs = refs[: len(held)], refs[len(held) :]
    freqs = query_ref.shape[0]
    _, width, channels = total_refs[0].shape
    extra = [
        columns_of(key_ref, block_of(axis, place), freqs, channels, width)
        for key_ref, place in zip(keys, places)
    ]
    copies, steps = [], []
    for f in range(span[0], span[0] + span[1]):
        used = [
            (key_ref, part[0], columns)
            for key_ref, part, columns in zip(keys, spans, extra)
            if holds(part, f)
        ]
        steps.append((f, used))

    def emit(i, f, sums):
        total = next(ref[f - part[0]] for ref, part in zip(total_refs, held) if holds(part, f))
        term = total + sums * (2.0 / width)
        if last:
            out_ref, result_ref, sems = out_refs
            result_ref[f] = term.T
            copies.append(pltpu.make_async_copy(result_ref.at[f], out_ref.at[f], sems.at[f]))
            copies[-1].start()
        else:
            out_refs[0][f - span[0]] = term

    band_sums(query_ref, steps, emit)
    for copy in copies:
        copy.wait()


def cost(shape, share):
    pairs = shape[0] * shape[1] * shape[1]
    return pl.CostEstimate(
        flops=share * pairs * shape[2], bytes_accessed=1 << 21, transcendentals=2 * pairs
    )


def chip_terms(shape, axis, low, own, pair, share):
    freqs, channels, width = shape
    whole = pl.BlockSpec(memory_space=pltpu.VMEM)
    return pl.pallas_call(
        functools.partial(chip_kernel, axis, low),
        out_shape=[
            jax.ShapeDtypeStruct((freqs, 2 * width, 2 * channels), jnp.bfloat16),
            jax.ShapeDtypeStruct((freqs, width, channels), jnp.float32),
        ],
        in_specs=[whole, whole],
        out_specs=[whole, whole],
        compiler_params=pltpu.CompilerParams(vmem_limit_bytes=vmem),
        cost_estimate=cost(shape, share),
    )(own, pair)


def band_terms(shape, axis, query, totals, keys, span, share, last=False):
    freqs, channels, width = shape
    whole = pl.BlockSpec(memory_space=pltpu.VMEM)
    out = shape if last else (span[1], width, channels)
    scratch = [pltpu.VMEM(shape, jnp.float32), pltpu.SemaphoreType.DMA((freqs,))]
    places, spans = tuple(key[1] for key in keys), tuple(key[2] for key in keys)
    held = tuple(total[1] for total in totals)
    return pl.pallas_call(
        functools.partial(band_kernel, axis, places, spans, held, span, last),
        out_shape=jax.ShapeDtypeStruct(out, jnp.float32),
        in_specs=[whole] * (1 + len(keys) + len(totals)),
        out_specs=pl.BlockSpec(memory_space=pl.ANY) if last else whole,
        scratch_shapes=scratch if last else [],
        compiler_params=pltpu.CompilerParams(vmem_limit_bytes=vmem),
        cost_estimate=cost(shape, share),
    )(query, *(key[0] for key in keys), *(total[0] for total in totals))


def local(axis, count, spectra, offsets, bins):
    shape = spectra.shape

    def fetched(value, place):
        sources = [(i + place[i % len(place)], i) for i in range(count)]
        return lax.ppermute(value, axis, [(i, t) for i, t in sources if 0 <= i < count])

    left = shape[0] // 2
    every, low, high = (0, shape[0]), (0, shape[0] - left), (shape[0] - left, left)
    own, own_low, own_high = pack(spectra, offsets, bins, (low[1], high[1]))
    near = fetched(own, NEAR)
    far = fetched(own, FAR)
    pair_low = fetched(own_low, PAIR)
    pair_high = fetched(own_high, PAIR)

    query, total = chip_terms(shape, axis, low[1], own, pair_low, shares[0])
    terms = functools.partial(band_terms, shape, axis, query)
    own_low, total = lax.optimization_barrier((own_low, total))
    cross_low = fetched(own_low, CROSS)
    rest = terms([(total, every)], [(pair_high, PAIR, high)], high, shares[1])
    own_high, rest = lax.optimization_barrier((own_high, rest))
    cross_high = fetched(own_high, CROSS)
    near, rest = lax.optimization_barrier((near, rest))
    near_pair = fetched(near, PAIR)
    total = terms([(rest, high), (total, every)], [(near, NEAR, every)], every, shares[2])
    total = terms([(total, every)], [(near_pair, NEAR_OF_PAIR, every)], every, shares[3])
    cross_high, total = lax.optimization_barrier((cross_high, total))
    high_pair = fetched(cross_high, PAIR)
    rest = terms([(total, every)], [(cross_high, CROSS, high)], high, shares[4])
    rest = terms([(rest, high)], [(high_pair, CROSS_OF_PAIR, high)], high, shares[5])
    cross_low, rest = lax.optimization_barrier((cross_low, rest))
    low_pair = fetched(cross_low, PAIR)
    first = terms([(total, every)], [(cross_low, CROSS, low)], low, shares[6])
    first = terms([(first, low)], [(low_pair, CROSS_OF_PAIR, low)], low, shares[7])
    far, first = lax.optimization_barrier((far, first))
    return terms([(first, low), (rest, high)], [(far, FAR, every)], every, shares[8], last=True)


def solution(mesh):
    (axis,) = mesh.axis_names
    return jax.shard_map(
        functools.partial(local, axis, mesh.shape[axis]),
        mesh=mesh,
        in_specs=(P(None, axis, None), P(axis), P()),
        out_specs=P(None, axis, None),
        check_vma=False,
    )
```

```python
import functools
import math

import jax
import jax.numpy as jnp
from jax import lax
from jax.experimental import pallas as pl
from jax.experimental.pallas import tpu as pltpu
from jax.sharding import PartitionSpec as P

spacing_metres = 8
period_metres = 4096
model_amp = 0.5
vmem = 24 << 20
shares = (64, 64, 64, 64, 64, 64, 64, 64, 64)

OWN = (0, 0, 0, 0)
PAIR = (1, -1, 1, -1)
NEAR = (2, 2, -2, -2)
CROSS = (-2, -2, 2, 2)
FAR = (-3, 3, -3, 3)
NEAR_OF_PAIR = (3, 1, -1, -3)
CROSS_OF_PAIR = (-1, -3, 3, 1)


def sine(steps):
    half, quarter = period_metres // 2, period_metres // 4
    turn = jnp.bitwise_and(steps + half, period_metres - 1) - half
    turn = jnp.where(turn > quarter, half - turn, jnp.where(turn < -quarter, -half - turn, turn))
    x = turn.astype(jnp.float32) * (2.0 * math.pi / period_metres)
    square = x * x
    total = jnp.full_like(x, -1.0 / math.factorial(11))
    for order in (9, 7, 5, 3, 1):
        total = total * square + (-1.0) ** (order // 2) / math.factorial(order)
    return total * x


def halves(value):
    high = value.astype(jnp.bfloat16).astype(jnp.float32)
    return high, value - high


def rows_of(freqs):
    return -(-2 * freqs // 8) * 8


def angles(tail_ref, block, freqs, channels):
    rows, width = rows_of(freqs), tail_ref.shape[1]
    row = lax.broadcasted_iota(jnp.int32, (rows, channels), 0)
    tail = tail_ref[...].astype(jnp.float32)
    lines = channels // width
    offsets = jnp.concatenate([tail[i : i + 1] for i in range(lines)], axis=1).astype(jnp.int32)
    factor = jnp.concatenate([tail[-rows:]] * lines, axis=1).astype(jnp.int32)
    channel = lax.broadcasted_iota(jnp.int32, (rows, channels), 1) + block * channels
    return factor * (channel * spacing_metres + offsets), row < freqs


def padded(parts, width):
    rows = jnp.concatenate(parts, axis=0)
    rest = jnp.zeros((width - rows.shape[0], rows.shape[1]), jnp.float32)
    return jnp.concatenate([rows, rest], axis=0)


def key_columns(tail_ref, block, freqs, channels, width):
    angle, is_cos = angles(tail_ref, block, freqs, channels)
    high, low = halves(sine(angle + jnp.where(is_cos, period_metres // 4, 0)))
    return padded([high, low, high, low], width).T.astype(jnp.bfloat16)


def query_rows(tail_ref, block, freqs, channels, width):
    angle, is_cos = angles(tail_ref, block, freqs, channels)
    quarter = period_metres // 4
    high, low = halves(-model_amp * sine(angle + jnp.where(is_cos, quarter, 0)))
    real = padded([high, high, low, low], width)
    high, low = halves(model_amp * sine(angle - jnp.where(is_cos, 0, quarter)))
    imag = padded([high, high, low, low], width)
    return real, imag


def turned(value):
    half = value.shape[0] // 2
    return jnp.concatenate([-value[half:], value[:half]], axis=0)


def block_of(axis, place):
    me = lax.axis_index(axis)
    kind = lax.rem(me, len(place))
    step = place[0]
    for i in range(1, len(place)):
        step = jnp.where(kind == i, place[i], step)
    return me + step


def pack_kernel(spectra_ref, off_ref, bins_ref, *refs):
    (own_ref, *part_refs), (off, bins, sems) = refs[:-3], refs[-3:]
    rows, width = spectra_ref.shape
    freqs, channels = bins_ref.shape[0], off.shape[1]
    lines, tail = channels // width, (own_ref.shape[0] - rows, width)
    sources, targets = [off_ref, bins_ref], [off, bins]
    for f in range(freqs):
        sources.append(spectra_ref.at[pl.ds(f * channels, channels)])
        targets.append(own_ref.at[pl.ds(f * channels, channels)])
    copies = [
        pltpu.make_async_copy(source, target, sems.at[i])
        for i, (source, target) in enumerate(zip(sources, targets))
    ]
    for copy in copies:
        copy.start()
    for copy in copies[:2]:
        copy.wait()
    row = lax.broadcasted_iota(jnp.int32, tail, 0)
    value = jnp.zeros(tail, jnp.int32)
    for i in range(lines):
        value = jnp.where(row == i, off[:, i * width : (i + 1) * width], value)
    first = tail[0] - rows_of(freqs)
    for f in range(freqs):
        value = jnp.where((row == first + f) | (row == first + freqs + f), bins[f], value)
    value = value.astype(jnp.float32).astype(jnp.bfloat16)
    for out_ref in (own_ref, *part_refs):
        out_ref[out_ref.shape[0] - tail[0] :, :] = value
    f = 0
    for part_ref in part_refs:
        for place in range((part_ref.shape[0] - tail[0]) // channels):
            copies[2 + f].wait()
            part_ref[place * channels : (place + 1) * channels, :] = own_ref[
                f * channels : (f + 1) * channels, :
            ]
            f += 1


def pack(spectra, offsets, bins, parts):
    freqs, channels, width = spectra.shape
    tail = -(-(channels // width + rows_of(freqs)) // 16) * 16
    whole = pl.BlockSpec(memory_space=pltpu.VMEM)
    return pl.pallas_call(
        pack_kernel,
        out_shape=[
            jax.ShapeDtypeStruct((part * channels + tail, width), spectra.dtype)
            for part in (freqs, *parts)
        ],
        in_specs=[pl.BlockSpec(memory_space=pltpu.HBM)] * 3,
        out_specs=[whole] * (1 + len(parts)),
        scratch_shapes=[
            pltpu.VMEM((1, channels), jnp.int32),
            pltpu.SMEM((freqs,), jnp.int32),
            pltpu.SemaphoreType.DMA((2 + freqs,)),
        ],
        compiler_params=pltpu.CompilerParams(vmem_limit_bytes=vmem),
        cost_estimate=pl.CostEstimate(flops=0, bytes_accessed=1 << 20, transcendentals=0),
    )(
        *(
            pltpu.with_memory_space_constraint(value, pltpu.HBM)
            for value in (spectra.reshape(freqs * channels, width), offsets.reshape(1, channels), bins)
        )
    )


def fill_queries(own_ref, query_ref, block):
    freqs, channels, width = query_ref.shape[0], query_ref.shape[2] // 2, own_ref.shape[1]
    tail_ref = own_ref.at[pl.ds(freqs * channels, own_ref.shape[0] - freqs * channels)]
    real, imag = query_rows(tail_ref, block, freqs, channels, width)
    row = lax.rem(lax.broadcasted_iota(jnp.int32, (width, channels), 0), rows_of(freqs))
    for f in range(freqs):
        own = own_ref[pl.ds(f * channels, channels), :].astype(jnp.float32).T * (2.0 / width)
        mine = (row == f) | (row == freqs + f)
        query_ref[f, :width, :channels] = own.astype(jnp.bfloat16)
        query_ref[f, :width, channels:] = (-turned(own)).astype(jnp.bfloat16)
        query_ref[f, width:, :channels] = jnp.where(mine, real, 0.0).astype(jnp.bfloat16)
        query_ref[f, width:, channels:] = jnp.where(mine, imag, 0.0).astype(jnp.bfloat16)


def spectra_of(f, keys):
    parts = []
    for ref, first, _ in keys:
        channels = keys[0][2].shape[0]
        parts.append(ref[pl.ds((f - first) * channels, channels), :])
    return parts[0] if len(parts) == 1 else jnp.concatenate(parts, axis=0)


def misfit_of(query_ref, f, keys):
    extra = [columns for _, _, columns in keys]
    extra = extra[0] if len(keys) == 1 else jnp.concatenate(extra, axis=0)
    key = jnp.concatenate([spectra_of(f, keys), extra], axis=1)
    return jnp.dot(key, query_ref[f], preferred_element_type=jnp.float32)


def band_sums(query_ref, steps, emit):
    channels = query_ref.shape[2] // 2
    ahead = misfit_of(query_ref, *steps[0])
    for i, (f, keys) in enumerate(steps):
        misfit = ahead
        if i + 1 < len(steps):
            ahead = misfit_of(query_ref, *steps[i + 1])
        grad = jnp.tanh(misfit).astype(jnp.bfloat16)
        sums = jnp.dot(spectra_of(f, keys).T, grad, preferred_element_type=jnp.float32)
        emit(i, f, sums[:, :channels] + turned(sums[:, channels:]))


def columns_of(key_ref, block, freqs, channels, width):
    tail = -(-(channels // width + rows_of(freqs)) // 16) * 16
    tail_ref = key_ref.at[pl.ds(key_ref.shape[0] - tail, tail)]
    return key_columns(tail_ref, block, freqs, channels, width)


def chip_kernel(axis, low, own_ref, pair_ref, query_ref, total_ref):
    freqs, width, channels = total_ref.shape
    own, pair = block_of(axis, OWN), block_of(axis, PAIR)
    fill_queries(own_ref, query_ref, own)
    own_columns = columns_of(own_ref, own, freqs, channels, width)
    pair_columns = columns_of(pair_ref, pair, freqs, channels, width)
    steps = []
    for f in range(freqs):
        steps.append((f, [(own_ref, 0, own_columns)]))
        if f < low:
            steps.append((f, [(pair_ref, 0, pair_columns)]))

    def emit(i, f, sums):
        if steps[i][1][0][0] is own_ref:
            total_ref[f] = sums * (4.0 / width)
        else:
            total_ref[f] += sums * (2.0 / width)

    band_sums(query_ref, steps, emit)


def holds(span, f):
    return span[0] <= f < span[0] + span[1]


def band_kernel(axis, places, spans, held, span, last, query_ref, *refs):
    keys, refs = refs[: len(places)], refs[len(places) :]
    total_refs, out_refs = refs[: len(held)], refs[len(held) :]
    freqs = query_ref.shape[0]
    _, width, channels = total_refs[0].shape
    extra = [
        columns_of(key_ref, block_of(axis, place), freqs, channels, width)
        for key_ref, place in zip(keys, places)
    ]
    copies, steps = [], []
    for f in range(span[0], span[0] + span[1]):
        used = [
            (key_ref, part[0], columns)
            for key_ref, part, columns in zip(keys, spans, extra)
            if holds(part, f)
        ]
        steps.append((f, used))

    def emit(i, f, sums):
        total = next(ref[f - part[0]] for ref, part in zip(total_refs, held) if holds(part, f))
        term = total + sums * (2.0 / width)
        if last:
            out_ref, result_ref, sems = out_refs
            result_ref[f] = term.T
            copies.append(pltpu.make_async_copy(result_ref.at[f], out_ref.at[f], sems.at[f]))
            copies[-1].start()
        else:
            out_refs[0][f - span[0]] = term

    band_sums(query_ref, steps, emit)
    for copy in copies:
        copy.wait()


def cost(shape, share):
    pairs = shape[0] * shape[1] * shape[1]
    return pl.CostEstimate(
        flops=share * pairs * shape[2], bytes_accessed=1 << 21, transcendentals=2 * pairs
    )


def chip_terms(shape, axis, low, own, pair, share):
    freqs, channels, width = shape
    whole = pl.BlockSpec(memory_space=pltpu.VMEM)
    return pl.pallas_call(
        functools.partial(chip_kernel, axis, low),
        out_shape=[
            jax.ShapeDtypeStruct((freqs, 2 * width, 2 * channels), jnp.bfloat16),
            jax.ShapeDtypeStruct((freqs, width, channels), jnp.float32),
        ],
        in_specs=[whole, whole],
        out_specs=[whole, whole],
        compiler_params=pltpu.CompilerParams(vmem_limit_bytes=vmem),
        cost_estimate=cost(shape, share),
    )(own, pair)


def band_terms(shape, axis, query, totals, keys, span, share, last=False):
    freqs, channels, width = shape
    whole = pl.BlockSpec(memory_space=pltpu.VMEM)
    out = shape if last else (span[1], width, channels)
    scratch = [pltpu.VMEM(shape, jnp.float32), pltpu.SemaphoreType.DMA((freqs,))]
    places, spans = tuple(key[1] for key in keys), tuple(key[2] for key in keys)
    held = tuple(total[1] for total in totals)
    return pl.pallas_call(
        functools.partial(band_kernel, axis, places, spans, held, span, last),
        out_shape=jax.ShapeDtypeStruct(out, jnp.float32),
        in_specs=[whole] * (1 + len(keys) + len(totals)),
        out_specs=pl.BlockSpec(memory_space=pl.ANY) if last else whole,
        scratch_shapes=scratch if last else [],
        compiler_params=pltpu.CompilerParams(vmem_limit_bytes=vmem),
        cost_estimate=cost(shape, share),
    )(query, *(key[0] for key in keys), *(total[0] for total in totals))


def local(axis, count, spectra, offsets, bins):
    shape = spectra.shape

    def fetched(value, place):
        sources = [(i + place[i % len(place)], i) for i in range(count)]
        return lax.ppermute(value, axis, [(i, t) for i, t in sources if 0 <= i < count])

    left = shape[0] // 2
    every, low, high = (0, shape[0]), (0, shape[0] - left), (shape[0] - left, left)
    own, own_low, own_high = pack(spectra, offsets, bins, (low[1], high[1]))
    near = fetched(own, NEAR)
    far = fetched(own, FAR)
    pair_low = fetched(own_low, PAIR)
    pair_high = fetched(own_high, PAIR)

    query, total = chip_terms(shape, axis, low[1], own, pair_low, shares[0])
    terms = functools.partial(band_terms, shape, axis, query)
    own_low, total = lax.optimization_barrier((own_low, total))
    cross_low = fetched(own_low, CROSS)
    rest = terms([(total, every)], [(pair_high, PAIR, high)], high, shares[1])
    own_high, rest = lax.optimization_barrier((own_high, rest))
    cross_high = fetched(own_high, CROSS)
    near, rest = lax.optimization_barrier((near, rest))
    near_pair = fetched(near, PAIR)
    total = terms([(rest, high), (total, every)], [(near, NEAR, every)], every, shares[2])
    total = terms([(total, every)], [(near_pair, NEAR_OF_PAIR, every)], every, shares[3])
    cross_high, total = lax.optimization_barrier((cross_high, total))
    high_pair = fetched(cross_high, PAIR)
    rest = terms([(total, every)], [(cross_high, CROSS, high)], high, shares[4])
    rest = terms([(rest, high)], [(high_pair, CROSS_OF_PAIR, high)], high, shares[5])
    cross_low, rest = lax.optimization_barrier((cross_low, rest))
    low_pair = fetched(cross_low, PAIR)
    first = terms([(total, every)], [(cross_low, CROSS, low)], low, shares[6])
    first = terms([(first, low)], [(low_pair, CROSS_OF_PAIR, low)], low, shares[7])
    far, first = lax.optimization_barrier((far, first))
    return terms([(first, low), (rest, high)], [(far, FAR, every)], every, shares[8], last=True)


def solution(mesh):
    (axis,) = mesh.axis_names
    return jax.shard_map(
        functools.partial(local, axis, mesh.shape[axis]),
        mesh=mesh,
        in_specs=(P(None, axis, None), P(axis), P()),
        out_specs=P(None, axis, None),
        check_vma=False,
    )
```

```python
import functools
import math

import jax
import jax.numpy as jnp
from jax import lax
from jax.experimental import pallas as pl
from jax.experimental.pallas import tpu as pltpu
from jax.sharding import PartitionSpec as P

spacing_metres = 8
period_metres = 4096
model_amp = 0.5
vmem = 24 << 20
chunk = 128
shares = (64, 64, 64, 64, 64, 64, 64, 64, 64)

OWN = (0, 0, 0, 0)
PAIR = (1, -1, 1, -1)
NEAR = (2, 2, -2, -2)
CROSS = (-2, -2, 2, 2)
FAR = (-3, 3, -3, 3)
NEAR_OF_PAIR = (3, 1, -1, -3)
CROSS_OF_PAIR = (-1, -3, 3, 1)


def sine(steps):
    half, quarter = period_metres // 2, period_metres // 4
    turn = jnp.bitwise_and(steps + half, period_metres - 1) - half
    turn = jnp.where(turn > quarter, half - turn, jnp.where(turn < -quarter, -half - turn, turn))
    x = turn.astype(jnp.float32) * (2.0 * math.pi / period_metres)
    square = x * x
    total = jnp.full_like(x, -1.0 / math.factorial(11))
    for order in (9, 7, 5, 3, 1):
        total = total * square + (-1.0) ** (order // 2) / math.factorial(order)
    return total * x


def halves(value):
    high = value.astype(jnp.bfloat16).astype(jnp.float32)
    return high, value - high


def rows_of(freqs):
    return -(-2 * freqs // 8) * 8


def angles(tail_ref, block, freqs, channels):
    rows, width = rows_of(freqs), tail_ref.shape[1]
    row = lax.broadcasted_iota(jnp.int32, (rows, channels), 0)
    tail = tail_ref[...].astype(jnp.float32)
    lines = channels // width
    offsets = jnp.concatenate([tail[i : i + 1] for i in range(lines)], axis=1).astype(jnp.int32)
    factor = jnp.concatenate([tail[-rows:]] * lines, axis=1).astype(jnp.int32)
    channel = lax.broadcasted_iota(jnp.int32, (rows, channels), 1) + block * channels
    return factor * (channel * spacing_metres + offsets), row < freqs


def padded(parts, width):
    rows = jnp.concatenate(parts, axis=0)
    rest = jnp.zeros((width - rows.shape[0], rows.shape[1]), jnp.float32)
    return jnp.concatenate([rows, rest], axis=0)


def key_columns(tail_ref, block, freqs, channels, width):
    angle, is_cos = angles(tail_ref, block, freqs, channels)
    high, low = halves(sine(angle + jnp.where(is_cos, period_metres // 4, 0)))
    rows = jnp.concatenate([high, low, high, low], axis=0)
    rest = jnp.zeros((channels, width - rows.shape[0]), jnp.float32)
    return jnp.concatenate([rows.T, rest], axis=1).astype(jnp.bfloat16)


def query_rows(tail_ref, block, freqs, channels, width):
    angle, is_cos = angles(tail_ref, block, freqs, channels)
    quarter = period_metres // 4
    high, low = halves(-model_amp * sine(angle + jnp.where(is_cos, quarter, 0)))
    real = padded([high, high, low, low], width)
    high, low = halves(model_amp * sine(angle - jnp.where(is_cos, 0, quarter)))
    imag = padded([high, high, low, low], width)
    return real, imag


def turned(value):
    half = value.shape[0] // 2
    return jnp.concatenate([-value[half:], value[:half]], axis=0)


def block_of(axis, place):
    me = lax.axis_index(axis)
    kind = lax.rem(me, len(place))
    step = place[0]
    for i in range(1, len(place)):
        step = jnp.where(kind == i, place[i], step)
    return me + step


def pack_kernel(spectra_ref, off_ref, bins_ref, *refs):
    (own_ref, *part_refs), (off, bins, sems) = refs[:-3], refs[-3:]
    rows, width = spectra_ref.shape
    freqs, channels = bins_ref.shape[0], off.shape[1]
    lines, tail = channels // width, (own_ref.shape[0] - rows, width)
    sources, targets = [off_ref, bins_ref], [off, bins]
    for f in range(freqs):
        sources.append(spectra_ref.at[pl.ds(f * channels, channels)])
        targets.append(own_ref.at[pl.ds(f * channels, channels)])
    copies = [
        pltpu.make_async_copy(source, target, sems.at[i])
        for i, (source, target) in enumerate(zip(sources, targets))
    ]
    for copy in copies:
        copy.start()
    for copy in copies[:2]:
        copy.wait()
    row = lax.broadcasted_iota(jnp.int32, tail, 0)
    value = jnp.zeros(tail, jnp.int32)
    for i in range(lines):
        value = jnp.where(row == i, off[:, i * width : (i + 1) * width], value)
    first = tail[0] - rows_of(freqs)
    for f in range(freqs):
        value = jnp.where((row == first + f) | (row == first + freqs + f), bins[f], value)
    value = value.astype(jnp.float32).astype(jnp.bfloat16)
    for out_ref in (own_ref, *part_refs):
        out_ref[out_ref.shape[0] - tail[0] :, :] = value
    f = 0
    for part_ref in part_refs:
        for place in range((part_ref.shape[0] - tail[0]) // channels):
            copies[2 + f].wait()
            part_ref[place * channels : (place + 1) * channels, :] = own_ref[
                f * channels : (f + 1) * channels, :
            ]
            f += 1


def pack(spectra, offsets, bins, parts):
    freqs, channels, width = spectra.shape
    tail = -(-(channels // width + rows_of(freqs)) // 16) * 16
    whole = pl.BlockSpec(memory_space=pltpu.VMEM)
    return pl.pallas_call(
        pack_kernel,
        out_shape=[
            jax.ShapeDtypeStruct((part * channels + tail, width), spectra.dtype)
            for part in (freqs, *parts)
        ],
        in_specs=[pl.BlockSpec(memory_space=pltpu.HBM)] * 3,
        out_specs=[whole] * (1 + len(parts)),
        scratch_shapes=[
            pltpu.VMEM((1, channels), jnp.int32),
            pltpu.SMEM((freqs,), jnp.int32),
            pltpu.SemaphoreType.DMA((2 + freqs,)),
        ],
        compiler_params=pltpu.CompilerParams(vmem_limit_bytes=vmem),
        cost_estimate=pl.CostEstimate(flops=0, bytes_accessed=1 << 20, transcendentals=0),
    )(
        *(
            pltpu.with_memory_space_constraint(value, pltpu.HBM)
            for value in (spectra.reshape(freqs * channels, width), offsets.reshape(1, channels), bins)
        )
    )


def fill_queries(own_ref, query_ref, block):
    freqs, channels, width = query_ref.shape[0], query_ref.shape[2] // 2, own_ref.shape[1]
    tail_ref = own_ref.at[pl.ds(freqs * channels, own_ref.shape[0] - freqs * channels)]
    real, imag = query_rows(tail_ref, block, freqs, channels, width)
    row = lax.rem(lax.broadcasted_iota(jnp.int32, (width, channels), 0), rows_of(freqs))
    for f in range(freqs):
        own = own_ref[pl.ds(f * channels, channels), :].astype(jnp.float32).T * (2.0 / width)
        mine = (row == f) | (row == freqs + f)
        query_ref[f, :width, :channels] = own.astype(jnp.bfloat16)
        query_ref[f, :width, channels:] = (-turned(own)).astype(jnp.bfloat16)
        query_ref[f, width:, :channels] = jnp.where(mine, real, 0.0).astype(jnp.bfloat16)
        query_ref[f, width:, channels:] = jnp.where(mine, imag, 0.0).astype(jnp.bfloat16)


def spectra_of(f, keys):
    parts = []
    for ref, first, _ in keys:
        channels = keys[0][2].shape[0]
        parts.append(ref[pl.ds((f - first) * channels, channels), :])
    return parts[0] if len(parts) == 1 else jnp.concatenate(parts, axis=0)


def misfit_of(query_ref, f, keys):
    extra = [columns for _, _, columns in keys]
    extra = extra[0] if len(keys) == 1 else jnp.concatenate(extra, axis=0)
    key = jnp.concatenate([spectra_of(f, keys), extra], axis=1)
    return jnp.dot(key, query_ref[f], preferred_element_type=jnp.float32)


def band_sums(query_ref, steps, emit):
    channels = query_ref.shape[2] // 2
    ahead = misfit_of(query_ref, *steps[0])
    for i, (f, keys) in enumerate(steps):
        misfit = ahead
        if i + 1 < len(steps):
            ahead = misfit_of(query_ref, *steps[i + 1])
        grad = jnp.tanh(misfit).astype(jnp.bfloat16)
        sums = jnp.dot(spectra_of(f, keys).T, grad, preferred_element_type=jnp.float32)
        emit(i, f, sums[:, :channels] + turned(sums[:, channels:]))


def columns_of(key_ref, block, freqs, channels, width):
    tail = -(-(channels // width + rows_of(freqs)) // 16) * 16
    tail_ref = key_ref.at[pl.ds(key_ref.shape[0] - tail, tail)]
    return key_columns(tail_ref, block, freqs, channels, width)


def chip_kernel(axis, low, own_ref, pair_ref, query_ref, total_ref):
    freqs, width, channels = total_ref.shape
    own, pair = block_of(axis, OWN), block_of(axis, PAIR)
    fill_queries(own_ref, query_ref, own)
    own_columns = columns_of(own_ref, own, freqs, channels, width)
    pair_columns = columns_of(pair_ref, pair, freqs, channels, width)
    steps = []
    for f in range(freqs):
        steps.append((f, [(own_ref, 0, own_columns)]))
        if f < low:
            steps.append((f, [(pair_ref, 0, pair_columns)]))

    def emit(i, f, sums):
        if steps[i][1][0][0] is own_ref:
            total_ref[f] = sums * (4.0 / width)
        else:
            total_ref[f] += sums * (2.0 / width)

    band_sums(query_ref, steps, emit)


def holds(span, f):
    return span[0] <= f < span[0] + span[1]


def band_kernel(axis, places, spans, held, span, last, query_ref, *refs):
    keys, refs = refs[: len(places)], refs[len(places) :]
    total_refs, out_refs = refs[: len(held)], refs[len(held) :]
    freqs = query_ref.shape[0]
    _, width, channels = total_refs[0].shape
    extra = [
        columns_of(key_ref, block_of(axis, place), freqs, channels, width)
        for key_ref, place in zip(keys, places)
    ]
    copies, steps = [], []
    for f in range(span[0], span[0] + span[1]):
        used = [
            (key_ref, part[0], columns)
            for key_ref, part, columns in zip(keys, spans, extra)
            if holds(part, f)
        ]
        steps.append((f, used))

    def emit(i, f, sums):
        total = next(ref[f - part[0]] for ref, part in zip(total_refs, held) if holds(part, f))
        term = total + sums * (2.0 / width)
        if last:
            out_ref, result_ref, sems = out_refs
            for start in range(0, channels, chunk):
                rows = pl.ds(start, chunk)
                result_ref[f, rows, :] = term[:, start : start + chunk].T
                copies.append(
                    pltpu.make_async_copy(
                        result_ref.at[f, rows], out_ref.at[f, rows], sems.at[len(copies)]
                    )
                )
                copies[-1].start()
        else:
            out_refs[0][f - span[0]] = term

    band_sums(query_ref, steps, emit)
    for copy in copies:
        copy.wait()


def cost(shape, share):
    pairs = shape[0] * shape[1] * shape[1]
    return pl.CostEstimate(
        flops=share * pairs * shape[2], bytes_accessed=1 << 21, transcendentals=2 * pairs
    )


def chip_terms(shape, axis, low, own, pair, share):
    freqs, channels, width = shape
    whole = pl.BlockSpec(memory_space=pltpu.VMEM)
    return pl.pallas_call(
        functools.partial(chip_kernel, axis, low),
        out_shape=[
            jax.ShapeDtypeStruct((freqs, 2 * width, 2 * channels), jnp.bfloat16),
            jax.ShapeDtypeStruct((freqs, width, channels), jnp.float32),
        ],
        in_specs=[whole, whole],
        out_specs=[whole, whole],
        compiler_params=pltpu.CompilerParams(vmem_limit_bytes=vmem),
        cost_estimate=cost(shape, share),
    )(own, pair)


def band_terms(shape, axis, query, totals, keys, span, share, last=False):
    freqs, channels, width = shape
    whole = pl.BlockSpec(memory_space=pltpu.VMEM)
    out = shape if last else (span[1], width, channels)
    scratch = [pltpu.VMEM(shape, jnp.float32), pltpu.SemaphoreType.DMA((freqs * (channels // chunk),))]
    places, spans = tuple(key[1] for key in keys), tuple(key[2] for key in keys)
    held = tuple(total[1] for total in totals)
    return pl.pallas_call(
        functools.partial(band_kernel, axis, places, spans, held, span, last),
        out_shape=jax.ShapeDtypeStruct(out, jnp.float32),
        in_specs=[whole] * (1 + len(keys) + len(totals)),
        out_specs=pl.BlockSpec(memory_space=pl.ANY) if last else whole,
        scratch_shapes=scratch if last else [],
        compiler_params=pltpu.CompilerParams(vmem_limit_bytes=vmem),
        cost_estimate=cost(shape, share),
    )(query, *(key[0] for key in keys), *(total[0] for total in totals))


def local(axis, count, spectra, offsets, bins):
    shape = spectra.shape

    def fetched(value, place):
        sources = [(i + place[i % len(place)], i) for i in range(count)]
        return lax.ppermute(value, axis, [(i, t) for i, t in sources if 0 <= i < count])

    left = shape[0] // 2
    every, low, high = (0, shape[0]), (0, shape[0] - left), (shape[0] - left, left)
    own, own_low, own_high = pack(spectra, offsets, bins, (low[1], high[1]))
    near = fetched(own, NEAR)
    far = fetched(own, FAR)
    pair_low = fetched(own_low, PAIR)
    pair_high = fetched(own_high, PAIR)

    query, total = chip_terms(shape, axis, low[1], own, pair_low, shares[0])
    terms = functools.partial(band_terms, shape, axis, query)
    own_low, total = lax.optimization_barrier((own_low, total))
    cross_low = fetched(own_low, CROSS)
    rest = terms([(total, every)], [(pair_high, PAIR, high)], high, shares[1])
    own_high, rest = lax.optimization_barrier((own_high, rest))
    cross_high = fetched(own_high, CROSS)
    near, rest = lax.optimization_barrier((near, rest))
    near_pair = fetched(near, PAIR)
    total = terms([(rest, high), (total, every)], [(near, NEAR, every)], every, shares[2])
    total = terms([(total, every)], [(near_pair, NEAR_OF_PAIR, every)], every, shares[3])
    cross_high, total = lax.optimization_barrier((cross_high, total))
    high_pair = fetched(cross_high, PAIR)
    rest = terms([(total, every)], [(cross_high, CROSS, high)], high, shares[4])
    rest = terms([(rest, high)], [(high_pair, CROSS_OF_PAIR, high)], high, shares[5])
    cross_low, rest = lax.optimization_barrier((cross_low, rest))
    low_pair = fetched(cross_low, PAIR)
    first = terms([(total, every)], [(cross_low, CROSS, low)], low, shares[6])
    first = terms([(first, low)], [(low_pair, CROSS_OF_PAIR, low)], low, shares[7])
    far, first = lax.optimization_barrier((far, first))
    return terms([(first, low), (rest, high)], [(far, FAR, every)], every, shares[8], last=True)


def solution(mesh):
    (axis,) = mesh.axis_names
    return jax.shard_map(
        functools.partial(local, axis, mesh.shape[axis]),
        mesh=mesh,
        in_specs=(P(None, axis, None), P(axis), P()),
        out_specs=P(None, axis, None),
        check_vma=False,
    )
```

```python
import functools
import math

import jax
import jax.numpy as jnp
from jax import lax
from jax.experimental import pallas as pl
from jax.experimental.pallas import tpu as pltpu
from jax.sharding import PartitionSpec as P

spacing_metres = 8
period_metres = 4096
model_amp = 0.5
vmem = 24 << 20
shares = (64, 64, 64, 64, 64, 64, 64, 64, 64)

OWN = (0, 0, 0, 0)
PAIR = (1, -1, 1, -1)
NEAR = (3, 1, -1, -3)
CROSS = (-2, -2, 2, 2)
FAR = (-3, 3, -3, 3)
NEAR_OF_PAIR = (2, 2, -2, -2)
CROSS_OF_PAIR = (-1, -3, 3, 1)


def sine(steps):
    half, quarter = period_metres // 2, period_metres // 4
    turn = jnp.bitwise_and(steps + half, period_metres - 1) - half
    turn = jnp.where(turn > quarter, half - turn, jnp.where(turn < -quarter, -half - turn, turn))
    x = turn.astype(jnp.float32) * (2.0 * math.pi / period_metres)
    square = x * x
    total = jnp.full_like(x, -1.0 / math.factorial(11))
    for order in (9, 7, 5, 3, 1):
        total = total * square + (-1.0) ** (order // 2) / math.factorial(order)
    return total * x


def halves(value):
    high = value.astype(jnp.bfloat16).astype(jnp.float32)
    return high, value - high


def rows_of(freqs):
    return -(-2 * freqs // 8) * 8


def angles(tail_ref, block, freqs, channels):
    rows, width = rows_of(freqs), tail_ref.shape[1]
    row = lax.broadcasted_iota(jnp.int32, (rows, channels), 0)
    tail = tail_ref[...].astype(jnp.float32)
    lines = channels // width
    offsets = jnp.concatenate([tail[i : i + 1] for i in range(lines)], axis=1).astype(jnp.int32)
    factor = jnp.concatenate([tail[-rows:]] * lines, axis=1).astype(jnp.int32)
    channel = lax.broadcasted_iota(jnp.int32, (rows, channels), 1) + block * channels
    return factor * (channel * spacing_metres + offsets), row < freqs


def padded(parts, width):
    rows = jnp.concatenate(parts, axis=0)
    rest = jnp.zeros((width - rows.shape[0], rows.shape[1]), jnp.float32)
    return jnp.concatenate([rows, rest], axis=0)


def key_columns(tail_ref, block, freqs, channels, width):
    angle, is_cos = angles(tail_ref, block, freqs, channels)
    high, low = halves(sine(angle + jnp.where(is_cos, period_metres // 4, 0)))
    return padded([high, low, high, low], width).T.astype(jnp.bfloat16)


def query_rows(tail_ref, block, freqs, channels, width):
    angle, is_cos = angles(tail_ref, block, freqs, channels)
    quarter = period_metres // 4
    high, low = halves(-model_amp * sine(angle + jnp.where(is_cos, quarter, 0)))
    real = padded([high, high, low, low], width)
    high, low = halves(model_amp * sine(angle - jnp.where(is_cos, 0, quarter)))
    imag = padded([high, high, low, low], width)
    return real, imag


def turned(value):
    half = value.shape[0] // 2
    return jnp.concatenate([-value[half:], value[:half]], axis=0)


def block_of(axis, place):
    me = lax.axis_index(axis)
    kind = lax.rem(me, len(place))
    step = place[0]
    for i in range(1, len(place)):
        step = jnp.where(kind == i, place[i], step)
    return me + step


def pack_kernel(spectra_ref, off_ref, bins_ref, *refs):
    (own_ref, *part_refs), (off, bins, sems) = refs[:-3], refs[-3:]
    rows, width = spectra_ref.shape
    freqs, channels = bins_ref.shape[0], off.shape[1]
    lines, tail = channels // width, (own_ref.shape[0] - rows, width)
    sources, targets = [off_ref, bins_ref], [off, bins]
    for f in range(freqs):
        sources.append(spectra_ref.at[pl.ds(f * channels, channels)])
        targets.append(own_ref.at[pl.ds(f * channels, channels)])
    copies = [
        pltpu.make_async_copy(source, target, sems.at[i])
        for i, (source, target) in enumerate(zip(sources, targets))
    ]
    for copy in copies:
        copy.start()
    for copy in copies[:2]:
        copy.wait()
    row = lax.broadcasted_iota(jnp.int32, tail, 0)
    value = jnp.zeros(tail, jnp.int32)
    for i in range(lines):
        value = jnp.where(row == i, off[:, i * width : (i + 1) * width], value)
    first = tail[0] - rows_of(freqs)
    for f in range(freqs):
        value = jnp.where((row == first + f) | (row == first + freqs + f), bins[f], value)
    value = value.astype(jnp.float32).astype(jnp.bfloat16)
    for out_ref in (own_ref, *part_refs):
        out_ref[out_ref.shape[0] - tail[0] :, :] = value
    f = 0
    for part_ref in part_refs:
        for place in range((part_ref.shape[0] - tail[0]) // channels):
            copies[2 + f].wait()
            part_ref[place * channels : (place + 1) * channels, :] = own_ref[
                f * channels : (f + 1) * channels, :
            ]
            f += 1


def pack(spectra, offsets, bins, parts):
    freqs, channels, width = spectra.shape
    tail = -(-(channels // width + rows_of(freqs)) // 16) * 16
    whole = pl.BlockSpec(memory_space=pltpu.VMEM)
    return pl.pallas_call(
        pack_kernel,
        out_shape=[
            jax.ShapeDtypeStruct((part * channels + tail, width), spectra.dtype)
            for part in (freqs, *parts)
        ],
        in_specs=[pl.BlockSpec(memory_space=pltpu.HBM)] * 3,
        out_specs=[whole] * (1 + len(parts)),
        scratch_shapes=[
            pltpu.VMEM((1, channels), jnp.int32),
            pltpu.SMEM((freqs,), jnp.int32),
            pltpu.SemaphoreType.DMA((2 + freqs,)),
        ],
        compiler_params=pltpu.CompilerParams(vmem_limit_bytes=vmem),
        cost_estimate=pl.CostEstimate(flops=0, bytes_accessed=1 << 20, transcendentals=0),
    )(
        *(
            pltpu.with_memory_space_constraint(value, pltpu.HBM)
            for value in (spectra.reshape(freqs * channels, width), offsets.reshape(1, channels), bins)
        )
    )


def fill_queries(own_ref, query_ref, block):
    freqs, channels, width = query_ref.shape[0], query_ref.shape[2] // 2, own_ref.shape[1]
    tail_ref = own_ref.at[pl.ds(freqs * channels, own_ref.shape[0] - freqs * channels)]
    real, imag = query_rows(tail_ref, block, freqs, channels, width)
    row = lax.rem(lax.broadcasted_iota(jnp.int32, (width, channels), 0), rows_of(freqs))
    for f in range(freqs):
        own = own_ref[pl.ds(f * channels, channels), :].astype(jnp.float32).T * (2.0 / width)
        mine = (row == f) | (row == freqs + f)
        query_ref[f, :width, :channels] = own.astype(jnp.bfloat16)
        query_ref[f, :width, channels:] = (-turned(own)).astype(jnp.bfloat16)
        query_ref[f, width:, :channels] = jnp.where(mine, real, 0.0).astype(jnp.bfloat16)
        query_ref[f, width:, channels:] = jnp.where(mine, imag, 0.0).astype(jnp.bfloat16)


def spectra_of(f, keys):
    parts = []
    for ref, first, _ in keys:
        channels = keys[0][2].shape[0]
        parts.append(ref[pl.ds((f - first) * channels, channels), :])
    return parts[0] if len(parts) == 1 else jnp.concatenate(parts, axis=0)


def misfit_of(query_ref, f, keys):
    extra = [columns for _, _, columns in keys]
    extra = extra[0] if len(keys) == 1 else jnp.concatenate(extra, axis=0)
    key = jnp.concatenate([spectra_of(f, keys), extra], axis=1)
    return jnp.dot(key, query_ref[f], preferred_element_type=jnp.float32)


def band_sums(query_ref, steps, emit):
    channels = query_ref.shape[2] // 2
    ahead = misfit_of(query_ref, *steps[0])
    for i, (f, keys) in enumerate(steps):
        misfit = ahead
        if i + 1 < len(steps):
            ahead = misfit_of(query_ref, *steps[i + 1])
        grad = jnp.tanh(misfit).astype(jnp.bfloat16)
        sums = jnp.dot(spectra_of(f, keys).T, grad, preferred_element_type=jnp.float32)
        emit(i, f, sums[:, :channels] + turned(sums[:, channels:]))


def columns_of(key_ref, block, freqs, channels, width):
    tail = -(-(channels // width + rows_of(freqs)) // 16) * 16
    tail_ref = key_ref.at[pl.ds(key_ref.shape[0] - tail, tail)]
    return key_columns(tail_ref, block, freqs, channels, width)


def chip_kernel(axis, low, own_ref, pair_ref, query_ref, total_ref):
    freqs, width, channels = total_ref.shape
    own, pair = block_of(axis, OWN), block_of(axis, PAIR)
    fill_queries(own_ref, query_ref, own)
    own_columns = columns_of(own_ref, own, freqs, channels, width)
    pair_columns = columns_of(pair_ref, pair, freqs, channels, width)
    steps = []
    for f in range(freqs):
        steps.append((f, [(own_ref, 0, own_columns)]))
        if f < low:
            steps.append((f, [(pair_ref, 0, pair_columns)]))

    def emit(i, f, sums):
        if steps[i][1][0][0] is own_ref:
            total_ref[f] = sums * (4.0 / width)
        else:
            total_ref[f] += sums * (2.0 / width)

    band_sums(query_ref, steps, emit)


def holds(span, f):
    return span[0] <= f < span[0] + span[1]


def band_kernel(axis, places, spans, held, span, last, query_ref, *refs):
    keys, refs = refs[: len(places)], refs[len(places) :]
    total_refs, out_refs = refs[: len(held)], refs[len(held) :]
    freqs = query_ref.shape[0]
    _, width, channels = total_refs[0].shape
    extra = [
        columns_of(key_ref, block_of(axis, place), freqs, channels, width)
        for key_ref, place in zip(keys, places)
    ]
    copies, steps = [], []
    for f in range(span[0], span[0] + span[1]):
        used = [
            (key_ref, part[0], columns)
            for key_ref, part, columns in zip(keys, spans, extra)
            if holds(part, f)
        ]
        steps.append((f, used))

    def emit(i, f, sums):
        total = next(ref[f - part[0]] for ref, part in zip(total_refs, held) if holds(part, f))
        term = total + sums * (2.0 / width)
        if last:
            out_ref, result_ref, sems = out_refs
            result_ref[f] = term.T
            copies.append(pltpu.make_async_copy(result_ref.at[f], out_ref.at[f], sems.at[f]))
            copies[-1].start()
        else:
            out_refs[0][f - span[0]] = term

    band_sums(query_ref, steps, emit)
    for copy in copies:
        copy.wait()


def cost(shape, share):
    pairs = shape[0] * shape[1] * shape[1]
    return pl.CostEstimate(
        flops=share * pairs * shape[2], bytes_accessed=1 << 21, transcendentals=2 * pairs
    )


def chip_terms(shape, axis, low, own, pair, share):
    freqs, channels, width = shape
    whole = pl.BlockSpec(memory_space=pltpu.VMEM)
    return pl.pallas_call(
        functools.partial(chip_kernel, axis, low),
        out_shape=[
            jax.ShapeDtypeStruct((freqs, 2 * width, 2 * channels), jnp.bfloat16),
            jax.ShapeDtypeStruct((freqs, width, channels), jnp.float32),
        ],
        in_specs=[whole, whole],
        out_specs=[whole, whole],
        compiler_params=pltpu.CompilerParams(vmem_limit_bytes=vmem),
        cost_estimate=cost(shape, share),
    )(own, pair)


def band_terms(shape, axis, query, totals, keys, span, share, last=False):
    freqs, channels, width = shape
    whole = pl.BlockSpec(memory_space=pltpu.VMEM)
    out = shape if last else (span[1], width, channels)
    scratch = [pltpu.VMEM(shape, jnp.float32), pltpu.SemaphoreType.DMA((freqs,))]
    places, spans = tuple(key[1] for key in keys), tuple(key[2] for key in keys)
    held = tuple(total[1] for total in totals)
    return pl.pallas_call(
        functools.partial(band_kernel, axis, places, spans, held, span, last),
        out_shape=jax.ShapeDtypeStruct(out, jnp.float32),
        in_specs=[whole] * (1 + len(keys) + len(totals)),
        out_specs=pl.BlockSpec(memory_space=pl.ANY) if last else whole,
        scratch_shapes=scratch if last else [],
        compiler_params=pltpu.CompilerParams(vmem_limit_bytes=vmem),
        cost_estimate=cost(shape, share),
    )(query, *(key[0] for key in keys), *(total[0] for total in totals))


def local(axis, count, spectra, offsets, bins):
    shape = spectra.shape

    def fetched(value, place):
        sources = [(i + place[i % len(place)], i) for i in range(count)]
        return lax.ppermute(value, axis, [(i, t) for i, t in sources if 0 <= i < count])

    left = shape[0] // 2
    every, low, high = (0, shape[0]), (0, shape[0] - left), (shape[0] - left, left)
    own, own_low, own_high = pack(spectra, offsets, bins, (low[1], high[1]))
    near = fetched(own, NEAR)
    far = fetched(own, FAR)
    pair_low = fetched(own_low, PAIR)
    pair_high = fetched(own_high, PAIR)

    query, total = chip_terms(shape, axis, low[1], own, pair_low, shares[0])
    terms = functools.partial(band_terms, shape, axis, query)
    own_low, total = lax.optimization_barrier((own_low, total))
    cross_low = fetched(own_low, CROSS)
    rest = terms([(total, every)], [(pair_high, PAIR, high)], high, shares[1])
    own_high, rest = lax.optimization_barrier((own_high, rest))
    cross_high = fetched(own_high, CROSS)
    near, rest = lax.optimization_barrier((near, rest))
    near_pair = fetched(near, PAIR)
    total = terms([(rest, high), (total, every)], [(near, NEAR, every)], every, shares[2])
    total = terms([(total, every)], [(near_pair, NEAR_OF_PAIR, every)], every, shares[3])
    cross_high, total = lax.optimization_barrier((cross_high, total))
    high_pair = fetched(cross_high, PAIR)
    rest = terms([(total, every)], [(cross_high, CROSS, high)], high, shares[4])
    rest = terms([(rest, high)], [(high_pair, CROSS_OF_PAIR, high)], high, shares[5])
    cross_low, rest = lax.optimization_barrier((cross_low, rest))
    low_pair = fetched(cross_low, PAIR)
    first = terms([(total, every)], [(cross_low, CROSS, low)], low, shares[6])
    first = terms([(first, low)], [(low_pair, CROSS_OF_PAIR, low)], low, shares[7])
    far, first = lax.optimization_barrier((far, first))
    return terms([(first, low), (rest, high)], [(far, FAR, every)], every, shares[8], last=True)


def solution(mesh):
    (axis,) = mesh.axis_names
    return jax.shard_map(
        functools.partial(local, axis, mesh.shape[axis]),
        mesh=mesh,
        in_specs=(P(None, axis, None), P(axis), P()),
        out_specs=P(None, axis, None),
        check_vma=False,
    )
```

```python
import functools
import math

import jax
import jax.numpy as jnp
from jax import lax
from jax.experimental import pallas as pl
from jax.experimental.pallas import tpu as pltpu
from jax.sharding import PartitionSpec as P

spacing_metres = 8
period_metres = 4096
model_amp = 0.5
vmem = 24 << 20
chunk = 128
shares = (64, 64, 64, 64, 64, 64, 64, 64, 64)

OWN = (0, 0, 0, 0)
PAIR = (1, -1, 1, -1)
NEAR = (3, 1, -1, -3)
CROSS = (-2, -2, 2, 2)
FAR = (-3, 3, -3, 3)
NEAR_OF_PAIR = (2, 2, -2, -2)
CROSS_OF_PAIR = (-1, -3, 3, 1)


def sine(steps):
    half, quarter = period_metres // 2, period_metres // 4
    turn = jnp.bitwise_and(steps + half, period_metres - 1) - half
    turn = jnp.where(turn > quarter, half - turn, jnp.where(turn < -quarter, -half - turn, turn))
    x = turn.astype(jnp.float32) * (2.0 * math.pi / period_metres)
    square = x * x
    total = jnp.full_like(x, -1.0 / math.factorial(11))
    for order in (9, 7, 5, 3, 1):
        total = total * square + (-1.0) ** (order // 2) / math.factorial(order)
    return total * x


def halves(value):
    high = value.astype(jnp.bfloat16).astype(jnp.float32)
    return high, value - high


def rows_of(freqs):
    return -(-2 * freqs // 8) * 8


def angles(tail_ref, block, freqs, channels):
    rows, width = rows_of(freqs), tail_ref.shape[1]
    row = lax.broadcasted_iota(jnp.int32, (rows, channels), 0)
    tail = tail_ref[...].astype(jnp.float32)
    lines = channels // width
    offsets = jnp.concatenate([tail[i : i + 1] for i in range(lines)], axis=1).astype(jnp.int32)
    factor = jnp.concatenate([tail[-rows:]] * lines, axis=1).astype(jnp.int32)
    channel = lax.broadcasted_iota(jnp.int32, (rows, channels), 1) + block * channels
    return factor * (channel * spacing_metres + offsets), row < freqs


def padded(parts, width):
    rows = jnp.concatenate(parts, axis=0)
    rest = jnp.zeros((width - rows.shape[0], rows.shape[1]), jnp.float32)
    return jnp.concatenate([rows, rest], axis=0)


def key_columns(tail_ref, block, freqs, channels, width):
    angle, is_cos = angles(tail_ref, block, freqs, channels)
    high, low = halves(sine(angle + jnp.where(is_cos, period_metres // 4, 0)))
    rows = jnp.concatenate([high, low, high, low], axis=0)
    rest = jnp.zeros((channels, width - rows.shape[0]), jnp.float32)
    return jnp.concatenate([rows.T, rest], axis=1).astype(jnp.bfloat16)


def query_rows(tail_ref, block, freqs, channels, width):
    angle, is_cos = angles(tail_ref, block, freqs, channels)
    quarter = period_metres // 4
    high, low = halves(-model_amp * sine(angle + jnp.where(is_cos, quarter, 0)))
    real = padded([high, high, low, low], width)
    high, low = halves(model_amp * sine(angle - jnp.where(is_cos, 0, quarter)))
    imag = padded([high, high, low, low], width)
    return real, imag


def turned(value):
    half = value.shape[0] // 2
    return jnp.concatenate([-value[half:], value[:half]], axis=0)


def block_of(axis, place):
    me = lax.axis_index(axis)
    kind = lax.rem(me, len(place))
    step = place[0]
    for i in range(1, len(place)):
        step = jnp.where(kind == i, place[i], step)
    return me + step


def pack_kernel(spectra_ref, off_ref, bins_ref, *refs):
    (own_ref, *part_refs), (off, bins, sems) = refs[:-3], refs[-3:]
    rows, width = spectra_ref.shape
    freqs, channels = bins_ref.shape[0], off.shape[1]
    lines, tail = channels // width, (own_ref.shape[0] - rows, width)
    sources, targets = [off_ref, bins_ref], [off, bins]
    for f in range(freqs):
        sources.append(spectra_ref.at[pl.ds(f * channels, channels)])
        targets.append(own_ref.at[pl.ds(f * channels, channels)])
    copies = [
        pltpu.make_async_copy(source, target, sems.at[i])
        for i, (source, target) in enumerate(zip(sources, targets))
    ]
    for copy in copies:
        copy.start()
    for copy in copies[:2]:
        copy.wait()
    row = lax.broadcasted_iota(jnp.int32, tail, 0)
    value = jnp.zeros(tail, jnp.int32)
    for i in range(lines):
        value = jnp.where(row == i, off[:, i * width : (i + 1) * width], value)
    first = tail[0] - rows_of(freqs)
    for f in range(freqs):
        value = jnp.where((row == first + f) | (row == first + freqs + f), bins[f], value)
    value = value.astype(jnp.float32).astype(jnp.bfloat16)
    for out_ref in (own_ref, *part_refs):
        out_ref[out_ref.shape[0] - tail[0] :, :] = value
    f = 0
    for part_ref in part_refs:
        for place in range((part_ref.shape[0] - tail[0]) // channels):
            copies[2 + f].wait()
            part_ref[place * channels : (place + 1) * channels, :] = own_ref[
                f * channels : (f + 1) * channels, :
            ]
            f += 1


def pack(spectra, offsets, bins, parts):
    freqs, channels, width = spectra.shape
    tail = -(-(channels // width + rows_of(freqs)) // 16) * 16
    whole = pl.BlockSpec(memory_space=pltpu.VMEM)
    return pl.pallas_call(
        pack_kernel,
        out_shape=[
            jax.ShapeDtypeStruct((part * channels + tail, width), spectra.dtype)
            for part in (freqs, *parts)
        ],
        in_specs=[pl.BlockSpec(memory_space=pltpu.HBM)] * 3,
        out_specs=[whole] * (1 + len(parts)),
        scratch_shapes=[
            pltpu.VMEM((1, channels), jnp.int32),
            pltpu.SMEM((freqs,), jnp.int32),
            pltpu.SemaphoreType.DMA((2 + freqs,)),
        ],
        compiler_params=pltpu.CompilerParams(vmem_limit_bytes=vmem),
        cost_estimate=pl.CostEstimate(flops=0, bytes_accessed=1 << 20, transcendentals=0),
    )(
        *(
            pltpu.with_memory_space_constraint(value, pltpu.HBM)
            for value in (spectra.reshape(freqs * channels, width), offsets.reshape(1, channels), bins)
        )
    )


def fill_queries(own_ref, query_ref, block):
    freqs, channels, width = query_ref.shape[0], query_ref.shape[2] // 2, own_ref.shape[1]
    tail_ref = own_ref.at[pl.ds(freqs * channels, own_ref.shape[0] - freqs * channels)]
    real, imag = query_rows(tail_ref, block, freqs, channels, width)
    row = lax.rem(lax.broadcasted_iota(jnp.int32, (width, channels), 0), rows_of(freqs))
    for f in range(freqs):
        own = own_ref[pl.ds(f * channels, channels), :].astype(jnp.float32).T * (2.0 / width)
        mine = (row == f) | (row == freqs + f)
        query_ref[f, :width, :channels] = own.astype(jnp.bfloat16)
        query_ref[f, :width, channels:] = (-turned(own)).astype(jnp.bfloat16)
        query_ref[f, width:, :channels] = jnp.where(mine, real, 0.0).astype(jnp.bfloat16)
        query_ref[f, width:, channels:] = jnp.where(mine, imag, 0.0).astype(jnp.bfloat16)


def spectra_of(f, keys):
    parts = []
    for ref, first, _ in keys:
        channels = keys[0][2].shape[0]
        parts.append(ref[pl.ds((f - first) * channels, channels), :])
    return parts[0] if len(parts) == 1 else jnp.concatenate(parts, axis=0)


def misfit_of(query_ref, f, keys):
    extra = [columns for _, _, columns in keys]
    extra = extra[0] if len(keys) == 1 else jnp.concatenate(extra, axis=0)
    key = jnp.concatenate([spectra_of(f, keys), extra], axis=1)
    return jnp.dot(key, query_ref[f], preferred_element_type=jnp.float32)


def band_sums(query_ref, steps, emit):
    channels = query_ref.shape[2] // 2
    ahead = misfit_of(query_ref, *steps[0])
    for i, (f, keys) in enumerate(steps):
        misfit = ahead
        if i + 1 < len(steps):
            ahead = misfit_of(query_ref, *steps[i + 1])
        grad = jnp.tanh(misfit).astype(jnp.bfloat16)
        sums = jnp.dot(spectra_of(f, keys).T, grad, preferred_element_type=jnp.float32)
        emit(i, f, sums[:, :channels] + turned(sums[:, channels:]))


def columns_of(key_ref, block, freqs, channels, width):
    tail = -(-(channels // width + rows_of(freqs)) // 16) * 16
    tail_ref = key_ref.at[pl.ds(key_ref.shape[0] - tail, tail)]
    return key_columns(tail_ref, block, freqs, channels, width)


def chip_kernel(axis, low, own_ref, pair_ref, query_ref, total_ref):
    freqs, width, channels = total_ref.shape
    own, pair = block_of(axis, OWN), block_of(axis, PAIR)
    fill_queries(own_ref, query_ref, own)
    own_columns = columns_of(own_ref, own, freqs, channels, width)
    pair_columns = columns_of(pair_ref, pair, freqs, channels, width)
    steps = []
    for f in range(freqs):
        steps.append((f, [(own_ref, 0, own_columns)]))
        if f < low:
            steps.append((f, [(pair_ref, 0, pair_columns)]))

    def emit(i, f, sums):
        if steps[i][1][0][0] is own_ref:
            total_ref[f] = sums * (4.0 / width)
        else:
            total_ref[f] += sums * (2.0 / width)

    band_sums(query_ref, steps, emit)


def holds(span, f):
    return span[0] <= f < span[0] + span[1]


def band_kernel(axis, places, spans, held, span, last, query_ref, *refs):
    keys, refs = refs[: len(places)], refs[len(places) :]
    total_refs, out_refs = refs[: len(held)], refs[len(held) :]
    freqs = query_ref.shape[0]
    _, width, channels = total_refs[0].shape
    extra = [
        columns_of(key_ref, block_of(axis, place), freqs, channels, width)
        for key_ref, place in zip(keys, places)
    ]
    copies, steps = [], []
    for f in range(span[0], span[0] + span[1]):
        used = [
            (key_ref, part[0], columns)
            for key_ref, part, columns in zip(keys, spans, extra)
            if holds(part, f)
        ]
        steps.append((f, used))

    def emit(i, f, sums):
        total = next(ref[f - part[0]] for ref, part in zip(total_refs, held) if holds(part, f))
        term = total + sums * (2.0 / width)
        if last:
            out_ref, result_ref, sems = out_refs
            for start in range(0, channels, chunk):
                rows = pl.ds(start, chunk)
                result_ref[f, rows, :] = term[:, start : start + chunk].T
                copies.append(
                    pltpu.make_async_copy(
                        result_ref.at[f, rows], out_ref.at[f, rows], sems.at[len(copies)]
                    )
                )
                copies[-1].start()
        else:
            out_refs[0][f - span[0]] = term

    band_sums(query_ref, steps, emit)
    for copy in copies:
        copy.wait()


def cost(shape, share):
    pairs = shape[0] * shape[1] * shape[1]
    return pl.CostEstimate(
        flops=share * pairs * shape[2], bytes_accessed=1 << 21, transcendentals=2 * pairs
    )


def chip_terms(shape, axis, low, own, pair, share):
    freqs, channels, width = shape
    whole = pl.BlockSpec(memory_space=pltpu.VMEM)
    return pl.pallas_call(
        functools.partial(chip_kernel, axis, low),
        out_shape=[
            jax.ShapeDtypeStruct((freqs, 2 * width, 2 * channels), jnp.bfloat16),
            jax.ShapeDtypeStruct((freqs, width, channels), jnp.float32),
        ],
        in_specs=[whole, whole],
        out_specs=[whole, whole],
        compiler_params=pltpu.CompilerParams(vmem_limit_bytes=vmem),
        cost_estimate=cost(shape, share),
    )(own, pair)


def band_terms(shape, axis, query, totals, keys, span, share, last=False):
    freqs, channels, width = shape
    whole = pl.BlockSpec(memory_space=pltpu.VMEM)
    out = shape if last else (span[1], width, channels)
    scratch = [pltpu.VMEM(shape, jnp.float32), pltpu.SemaphoreType.DMA((freqs * (channels // chunk),))]
    places, spans = tuple(key[1] for key in keys), tuple(key[2] for key in keys)
    held = tuple(total[1] for total in totals)
    return pl.pallas_call(
        functools.partial(band_kernel, axis, places, spans, held, span, last),
        out_shape=jax.ShapeDtypeStruct(out, jnp.float32),
        in_specs=[whole] * (1 + len(keys) + len(totals)),
        out_specs=pl.BlockSpec(memory_space=pl.ANY) if last else whole,
        scratch_shapes=scratch if last else [],
        compiler_params=pltpu.CompilerParams(vmem_limit_bytes=vmem),
        cost_estimate=cost(shape, share),
    )(query, *(key[0] for key in keys), *(total[0] for total in totals))


def local(axis, count, spectra, offsets, bins):
    shape = spectra.shape

    def fetched(value, place):
        sources = [(i + place[i % len(place)], i) for i in range(count)]
        return lax.ppermute(value, axis, [(i, t) for i, t in sources if 0 <= i < count])

    left = shape[0] // 2
    every, low, high = (0, shape[0]), (0, shape[0] - left), (shape[0] - left, left)
    own, own_low, own_high = pack(spectra, offsets, bins, (low[1], high[1]))
    near = fetched(own, NEAR)
    far = fetched(own, FAR)
    pair_low = fetched(own_low, PAIR)
    pair_high = fetched(own_high, PAIR)

    query, total = chip_terms(shape, axis, low[1], own, pair_low, shares[0])
    terms = functools.partial(band_terms, shape, axis, query)
    own_low, total = lax.optimization_barrier((own_low, total))
    cross_low = fetched(own_low, CROSS)
    rest = terms([(total, every)], [(pair_high, PAIR, high)], high, shares[1])
    own_high, rest = lax.optimization_barrier((own_high, rest))
    cross_high = fetched(own_high, CROSS)
    near, rest = lax.optimization_barrier((near, rest))
    near_pair = fetched(near, PAIR)
    total = terms([(rest, high), (total, every)], [(near, NEAR, every)], every, shares[2])
    total = terms([(total, every)], [(near_pair, NEAR_OF_PAIR, every)], every, shares[3])
    cross_high, total = lax.optimization_barrier((cross_high, total))
    high_pair = fetched(cross_high, PAIR)
    rest = terms([(total, every)], [(cross_high, CROSS, high)], high, shares[4])
    rest = terms([(rest, high)], [(high_pair, CROSS_OF_PAIR, high)], high, shares[5])
    cross_low, rest = lax.optimization_barrier((cross_low, rest))
    low_pair = fetched(cross_low, PAIR)
    first = terms([(total, every)], [(cross_low, CROSS, low)], low, shares[6])
    first = terms([(first, low)], [(low_pair, CROSS_OF_PAIR, low)], low, shares[7])
    far, first = lax.optimization_barrier((far, first))
    return terms([(first, low), (rest, high)], [(far, FAR, every)], every, shares[8], last=True)


def solution(mesh):
    (axis,) = mesh.axis_names
    return jax.shard_map(
        functools.partial(local, axis, mesh.shape[axis]),
        mesh=mesh,
        in_specs=(P(None, axis, None), P(axis), P()),
        out_specs=P(None, axis, None),
        check_vma=False,
    )
```
